128 devices in a mesh: subj: 16 (over y, z_lo, core), slab: 8 (over z_hi, x).
Axes of the slice: x: 4, y: 4, z: 4 (z_hi: 2, z_lo: 2; z = z_hi * 2 + z_lo), core: 2. Of those that a mesh axis runs over, the one named last changes fastest.
Arguments:
- template: float32 [8, 4096, 128], P('slab', 'subj'), may hold values from -6 to 6
- subject: bfloat16 [16, 8, 256, 128], P('subj', 'slab'), may hold values from -6 to 6
- tile_lists: int32 [16, 8, 4, 256], P('subj', 'slab'), may hold values from 0 to 4105, as said below
- corners: int32 [16, 8, 256, 8, 128], P('subj', 'slab'), may hold values from 0 to 511, as said below
- fractions: float32 [16, 8, 256, 3, 128], P('subj', 'slab'), may hold values from 0 to 1
- live_tiles: int32 [16, 8], P('subj', 'slab'), may hold values from 32 to 256, as said below
Outputs:
- new_atlas: float32 [8, 4096, 128], P('slab', 'subj')
- correlation: float32 [16, 8, 256], P('subj', 'slab')
The draws below stay inside these ranges and needn't reach their ends.
Inputs may be any that keep to these rules, and one draw needn't show every extreme that they name: `tile_lists`: warped tile t lists base, base + 1, base + 8, base + 9 for one base from 0 to 4096; in every subject and slab warped tile 0 has base 0 and warped tile 1 has base 4096. The eight corners of a voxel are start + 0, 1, 4, 5, 16, 17, 20, 21 for one start a voxel, corner q adding 1, 4 and 16 for its bits 0, 1 and 2, so they are distinct. `live_tiles`: each entry is 256, 128, 64 or 32.
All inputs are finite; a program needn't handle non-finite values.
Results may differ from the reference program's by a relative error of at most 0.0014.
Values may be sent and summed in bfloat16 or wider, within the bound.
No kernel may reach another device: no remote copies, remote signals or barrier semaphores. Data moves between devices by JAX's collectives and lax.ppermute only.
A program may use at most 128 MiB of HBM per device.

```python
import jax
import jax.numpy as jnp
from jax import lax

TILE = 128
SLOTS = 4
ROW = 8
ITERS = 2
WT = 256
HALO = 5
SUBJECTS = 16
SLABS = 8
TS = 4096


def draw_tile_lists(key, part):
    base_tiles = jax.random.randint(jax.random.fold_in(key, 11), (SUBJECTS, SLABS, WT), 0, TS + 1, dtype=jnp.int32)
    base_tiles = base_tiles.at[:, :, 0].set(0)
    base_tiles = base_tiles.at[:, :, 1].set(TS)
    offsets = jnp.array([0, 1, ROW, ROW + 1], dtype=jnp.int32)
    return base_tiles[:, :, None, :] + offsets[None, None, :, None]


def draw_corners(key, part):
    starts = jax.random.randint(jax.random.fold_in(key, 23), (SUBJECTS, SLABS, WT, TILE), 0, SLOTS * TILE - 21, dtype=jnp.int32)
    starts = starts.at[:, :, 0, 0].set(SLOTS * TILE - 22)
    starts = starts.at[:, :, 0, 1].set(0)
    offsets = jnp.array([0, 1, 4, 5, 16, 17, 20, 21], dtype=jnp.int32)
    return starts[:, :, :, None, :] + offsets[None, None, None, :, None]


def draw_live_tiles(key, part):
    shifts = jax.random.randint(jax.random.fold_in(key, 31), (SUBJECTS * SLABS,), 0, 4, dtype=jnp.int32)
    counts = jnp.right_shift(jnp.full((SUBJECTS * SLABS,), WT, jnp.int32), shifts)
    spots = jax.random.permutation(jax.random.fold_in(key, 37), SUBJECTS * SLABS)
    counts = counts.at[spots[0]].set(WT)
    counts = counts.at[spots[1]].set(WT // 8)
    return counts.reshape(SUBJECTS, SLABS)


def level_of(own_key, dims, split, low, top_value):
    factor_of, own = 1.0, jax.random.fold_in(own_key, 6)
    for position, shards_of in split:
        draws = jnp.exp(jax.random.uniform(jax.random.fold_in(own, position), (shards_of,), jnp.float32, low / len(split), top_value / len(split)))
        factor_of = factor_of * jnp.repeat(draws, dims[position] // shards_of).reshape([-1 if axis == position else 1 for axis in range(len(dims))])
    return factor_of


def normal_values(rng, dims, width, bound, pieces=(), kind=jnp.bfloat16):
    values = width * jax.random.normal(rng, dims, jnp.float32)
    if pieces:
        values = values * level_of(rng, dims, pieces, -0.22, 0.18)
    return jnp.clip(values, -bound, bound).astype(kind)


def setup_inputs(seed: int = 0) -> dict:
    keys = jax.random.split(jax.random.key(seed), 7)
    return {
        "template": normal_values(keys[0], (SLABS, TS, TILE), 1.0, 6.0, ((0, 8), (1, 16)), jnp.float32),
        "subject": normal_values(keys[1], (SUBJECTS, SLABS, WT, TILE), 1.0, 6.0, ((0, 16), (1, 8))),
        "tile_lists": draw_tile_lists(jax.random.fold_in(keys[6], 71), 0),
        "corners": draw_corners(jax.random.fold_in(keys[6], 71), 0),
        "fractions": jnp.clip(1.0 * jax.random.uniform(keys[4], (SUBJECTS, SLABS, WT, 3, TILE), jnp.float32) ** level_of(keys[4], (SUBJECTS, SLABS, WT, 3, TILE), ((0, 16), (1, 8)), -0.2, 0.2), 0.0, 1.0),
        "live_tiles": draw_live_tiles(jax.random.fold_in(keys[6], 71), 0),
    }


epsilon = 1e-05
ascent = 40.0

def corner_weights(fractions):
    along_x = fractions[..., 0, :]
    along_y = fractions[..., 1, :]
    along_z = fractions[..., 2, :]
    stacked = []
    for corner in range(8):
        factor_x = along_x if corner & 1 else 1.0 - along_x
        factor_y = along_y if corner & 2 else 1.0 - along_y
        factor_z = along_z if corner & 4 else 1.0 - along_z
        stacked.append(factor_x * factor_y * factor_z)
    return jnp.stack(stacked, axis=-2)

def splat_row(values, indices):
    return jax.ops.segment_sum(values, indices, SLOTS * TILE)

def reference(template, subject, tile_lists, corners, fractions, live_tiles):
    weights = corner_weights(fractions.astype(jnp.float32)).astype(jnp.bfloat16)
    weight_wide = weights.astype(jnp.float32)
    target = subject.astype(jnp.float32)
    centered = target - lax.optimization_barrier(jnp.mean(target, axis=-1, keepdims=True))
    subject_var = lax.optimization_barrier(jnp.mean(centered * centered, axis=-1)) + epsilon
    is_alive = jnp.arange(WT, dtype=jnp.int32)[None, None, :] < live_tiles[:, :, None]
    band_rows = jnp.arange(SLABS, dtype=jnp.int32)[None, :, None, None] * TS + tile_lists
    band_rows = jnp.transpose(band_rows, (0, 1, 3, 2))
    flat_corners = corners.reshape(SUBJECTS, SLABS, WT, 8 * TILE)

    def iterate(atlas_now):
        padded = jnp.pad(atlas_now.astype(jnp.bfloat16).reshape(SLABS * TS, TILE), ((HALO, HALO), (0, 0)))
        footing = padded[band_rows].reshape(SUBJECTS, SLABS, WT, SLOTS * TILE)
        picked = jnp.take_along_axis(footing, flat_corners, axis=-1).reshape(SUBJECTS, SLABS, WT, 8, TILE)
        warped = lax.optimization_barrier(jnp.sum(weight_wide * picked.astype(jnp.float32), axis=3))
        deviation = warped - lax.optimization_barrier(jnp.mean(warped, axis=-1, keepdims=True))
        warp_var = lax.optimization_barrier(jnp.mean(deviation * deviation, axis=-1)) + epsilon
        scale = jnp.sqrt(warp_var * subject_var)
        correl = lax.optimization_barrier(jnp.mean(deviation * centered, axis=-1)) / scale
        slopes = (centered / scale[..., None] - correl[..., None] * deviation / warp_var[..., None]) / TILE
        slopes = jnp.where(is_alive[..., None], slopes, 0.0).astype(jnp.bfloat16)
        correl = jnp.where(is_alive, correl, 0.0)
        splats = weight_wide * slopes.astype(jnp.float32)[:, :, :, None, :]
        contrib = jax.vmap(splat_row)(splats.reshape(-1, 8 * TILE), flat_corners.reshape(-1, 8 * TILE))
        grad_pad = jnp.zeros((SLABS * TS + 2 * HALO, TILE), jnp.float32)
        grad_pad = grad_pad.at[band_rows.reshape(-1)].add(contrib.reshape(-1, TILE))
        ascent_dir = grad_pad[HALO:HALO + SLABS * TS].reshape(SLABS, TS, TILE)
        return (atlas_now + ascent * ascent_dir, correl)
    atlas_now = template
    correl = jnp.zeros((SUBJECTS, SLABS, WT), jnp.float32)
    for rounds in range(ITERS):
        atlas_now, correl = iterate(atlas_now)
    return (atlas_now, correl)
```

```python
import jax
import jax.numpy as jnp
from jax import lax
from jax.experimental import pallas as pl
from jax.experimental.pallas import tpu as pltpu
from jax.sharding import PartitionSpec as P

TILE = 128
SLOTS = 4
ROW = 8
ITERS = 2
HALO = 5
RIM = 8
CAP = 36
PAD = 40
META = 3 * CAP
BLOCK = 3 * CAP + 4
COUNT_AT = 126
MOST_AT = 127
FRAC_UNIT = 65535.0
U_UNIT = float(2**27)
STEP = 32

epsilon = 1e-05
ascent = 40.0

SPOTS = (0, 1, ROW, ROW + 1)
SHIFTS = (0, 1, 4, 5)


def pieces_of(word):
    return [
        ((word >> shift) & 255).astype(jnp.float32).astype(jnp.bfloat16) for shift in (0, 8, 16, 24)
    ]


def pack_kernel(own_rows, live_ref, round_ref, lists_ref, corners_ref, fractions_ref, subject_ref, send_ref, slot_ref):
    groups = send_ref.shape[0] // BLOCK
    tiles = subject_ref.shape[0]
    base = lists_ref[0:1, :]
    alive = lax.broadcasted_iota(jnp.int32, (1, tiles), 1) < live_ref[0, 0]
    owner = jnp.minimum(base // own_rows, groups - 1)
    local = base - owner * own_rows
    group_iota = lax.broadcasted_iota(jnp.int32, (groups, tiles), 0)
    member = jnp.where((group_iota == owner) & alive, 1.0, 0.0)
    before = lax.broadcasted_iota(jnp.int32, (tiles, tiles), 0) < lax.broadcasted_iota(
        jnp.int32, (tiles, tiles), 1
    )
    earlier = jnp.dot(
        member.astype(jnp.bfloat16),
        jnp.where(before, 1.0, 0.0).astype(jnp.bfloat16),
        preferred_element_type=jnp.float32,
    )
    counts = jnp.sum(member, axis=1, keepdims=True)
    first = round_ref[0, 0] * CAP
    rank = jnp.sum(member * earlier, axis=0, keepdims=True).astype(jnp.int32) - first
    chosen = alive & (rank >= 0) & (rank < CAP)
    slot = jnp.where(chosen, owner * PAD + rank, -1)
    slot_ref[...] = slot
    pick = jnp.where(
        lax.broadcasted_iota(jnp.int32, (groups * PAD, tiles), 0) == slot, 1.0, 0.0
    ).astype(jnp.bfloat16)

    at_rank = jnp.where(
        (lax.broadcasted_iota(jnp.int32, (TILE, tiles), 0) == rank) & chosen, 1.0, 0.0
    ).astype(jnp.bfloat16)
    local_high = (member * (local >> 4).astype(jnp.float32)).astype(jnp.bfloat16)
    local_low = (member * (local & 15).astype(jnp.float32)).astype(jnp.bfloat16)
    across = (((1,), (1,)), ((), ()))
    bases = 16.0 * lax.dot_general(
        local_high, at_rank, across, preferred_element_type=jnp.float32
    ) + lax.dot_general(local_low, at_rank, across, preferred_element_type=jnp.float32)
    here = jnp.clip(counts.astype(jnp.int32) - first, 0, CAP)
    most = jnp.max(counts, axis=0, keepdims=True).astype(jnp.int32)
    lane = lax.broadcasted_iota(jnp.int32, (groups, TILE), 1)
    header = jnp.where(
        lane == COUNT_AT, here, jnp.where(lane == MOST_AT, most, bases.astype(jnp.int32))
    )

    target = subject_ref[...].astype(jnp.float32)
    centered = target - jnp.mean(target, axis=-1, keepdims=True)
    subject_var = jnp.mean(centered * centered, axis=-1, keepdims=True) + epsilon
    unit = centered / jnp.sqrt(subject_var)
    coded = [
        (fractions_ref[d] * FRAC_UNIT + 0.5).astype(jnp.int32) for d in range(3)
    ]
    words = (
        coded[0] | (coded[1] << 16),
        coded[2] | (corners_ref[:, 0, :] << 16),
        jnp.round(unit * U_UNIT).astype(jnp.int32),
    )
    for w, word in enumerate(words):
        data = jnp.concatenate(pieces_of(word), axis=1)
        moved = jnp.dot(pick, data, preferred_element_type=jnp.float32)
        low = (moved[:, :TILE] + 256.0 * moved[:, TILE : 2 * TILE]).astype(jnp.int32)
        high = (moved[:, 2 * TILE : 3 * TILE] + 256.0 * moved[:, 3 * TILE :]).astype(jnp.int32)
        whole = low | (high << 16)
        for g in range(groups):
            send_ref[pl.ds(g * BLOCK + w * CAP, CAP), :] = whole[g * PAD : g * PAD + CAP]
    for g in range(groups):
        send_ref[pl.ds(g * BLOCK + META, 4), :] = jnp.broadcast_to(header[g : g + 1], (4, TILE))


def compact(meta_ref, groups, base_of, from_row, slot_of):
    def source(s, state):
        def take(r, place):
            base_of[place] = meta_ref[s, r] + (RIM - HALO)
            from_row[place] = s * BLOCK + r
            slot_of[place] = s * CAP + r
            return place + 1

        place = lax.fori_loop(0, meta_ref[s, COUNT_AT], take, state[0])
        return place, jnp.maximum(state[1], meta_ref[s, MOST_AT])

    total, most = lax.fori_loop(0, groups, source, (jnp.int32(0), jnp.int32(0)))
    for extra in range(8):
        base_of[total + extra] = 0
        from_row[total + extra] = 0
        slot_of[total + extra] = groups * CAP
    return total, (most + (CAP - 1)) // CAP


def fetch(total, recv_ref, from_row, words, table, base_of, foot):
    def body(step, carry):
        at = pl.multiple_of(step * 8, 8)
        for i in range(8):
            here = pl.ds(at + i, 1)
            if recv_ref is not None:
                row = from_row[at + i]
                for w in range(3):
                    words[w, here, :] = recv_ref[pl.ds(row + w * CAP, 1), :]
            base = base_of[at + i]
            for k, shift in enumerate(SPOTS):
                foot[k, here, :] = table[pl.ds(base + shift, 1), :]
        return carry

    lax.fori_loop(0, (total + 7) // 8, body, 0)


def fractions_of(first, second):
    return (
        (first & 65535).astype(jnp.float32) * (1.0 / FRAC_UNIT),
        lax.shift_right_logical(first, 16).astype(jnp.float32) * (1.0 / FRAC_UNIT),
        (second & 65535).astype(jnp.float32) * (1.0 / FRAC_UNIT),
    )


def weights_of(along):
    away = [1.0 - x for x in along]
    found = []
    for q in range(8):
        weight = (
            (along[0] if q & 1 else away[0])
            * (along[1] if q & 2 else away[1])
            * (along[2] if q & 4 else away[2])
        )
        found.append(weight.astype(jnp.bfloat16).astype(jnp.float32))
    return found


def sample(total, words, foot, give):
    def body(step, carry):
        at = pl.multiple_of(step * STEP, STEP)
        here = pl.ds(at, STEP)
        second = words[1, here, :]
        unit = words[2, here, :].astype(jnp.float32) * (1.0 / U_UNIT)
        start = lax.shift_right_logical(second, 16)
        tables = [foot[k, here, :] for k in range(SLOTS)]
        weights = weights_of(fractions_of(words[0, here, :], second))
        warped = None
        for q in range(8):
            column = start + (SHIFTS[q & 3] + (16 if q & 4 else 0))
            lane = column & (TILE - 1)
            tile = column >> 7
            got = [
                jnp.take_along_axis(t, lane, axis=1, mode="promise_in_bounds") for t in tables
            ]
            picked = jnp.where(
                tile < 2, jnp.where(tile < 1, got[0], got[1]), jnp.where(tile < 3, got[2], got[3])
            )
            term = weights[q] * picked
            warped = term if warped is None else warped + term
        deviation = warped - jnp.mean(warped, axis=-1, keepdims=True)
        warp_var = jnp.mean(deviation * deviation, axis=-1, keepdims=True) + epsilon
        inverse = 1.0 / jnp.sqrt(warp_var)
        correl = jnp.mean(deviation * unit, axis=-1, keepdims=True) * inverse
        slope = (unit * inverse - (correl / warp_var) * deviation) * (1.0 / TILE)
        alive = at + lax.broadcasted_iota(jnp.int32, (STEP, TILE), 0) < total
        slope = jnp.where(alive, slope, 0.0).astype(jnp.bfloat16).astype(jnp.float32)
        give(here, weights, start, slope, jnp.broadcast_to(correl, (STEP, TILE)))
        return carry

    lax.fori_loop(0, (total + (STEP - 1)) // STEP, body, 0)


def send_back(total, rows, slot_of, correl_ref):
    def body(step, carry):
        at = pl.multiple_of(step * 8, 8)
        for i in range(8):
            correl_ref[pl.ds(slot_of[at + i], 1), :] = rows[pl.ds(at + i, 1), :]
        return carry

    lax.fori_loop(0, (total + 7) // 8, body, 0)


def splat_all(total, starts, values, base_of, acc):
    acc[...] = jnp.zeros(acc.shape, jnp.float32)
    high_iota = lax.broadcasted_iota(jnp.int32, (32, TILE), 0)
    low_iota = lax.broadcasted_iota(jnp.int32, (16, TILE), 0)
    across = (((1,), (1,)), ((), ()))

    def body(step, carry):
        at = pl.multiple_of(step * 8, 8)
        for i in range(8):
            line = pl.ds(at + i, 1)
            start = starts[line, :]
            high = high_iota - (start >> 4)
            low = low_iota - (start & 15)
            ones = [jnp.where(high == j, 1.0, 0.0).astype(jnp.bfloat16) for j in range(3)]
            near = [jnp.broadcast_to(values[q, line, :], (16, TILE)) for q in range(4)]
            far = [jnp.broadcast_to(values[q + 4, line, :], (16, TILE)) for q in range(4)]
            inside = [low == shift for shift in SHIFTS]
            wrapped = [low == shift - 16 for shift in SHIFTS]
            parts = [jnp.zeros((16, TILE), jnp.float32) for _ in range(3)]
            for q in range(4):
                parts[0] = jnp.where(inside[q], near[q], parts[0])
                parts[1] = jnp.where(inside[q], far[q], parts[1])
                if q > 0:
                    parts[1] = jnp.where(wrapped[q], near[q], parts[1])
                    parts[2] = jnp.where(wrapped[q], far[q], parts[2])
            splat = None
            for j in range(3):
                coarse = parts[j].astype(jnp.bfloat16)
                fine = (parts[j] - coarse.astype(jnp.float32)).astype(jnp.bfloat16)
                term = lax.dot_general(
                    ones[j],
                    jnp.concatenate([coarse, fine], axis=0),
                    across,
                    preferred_element_type=jnp.float32,
                )
                splat = term if splat is None else splat + term
            base = base_of[at + i]
            spots = [pl.ds(pl.multiple_of((base + shift) * 8, 8), 8) for shift in SPOTS]
            sums = [acc[spots[k], 0:32] + splat[8 * k : 8 * k + 8] for k in range(SLOTS)]
            for k in range(SLOTS):
                acc[spots[k], 0:32] = sums[k]
        return carry

    lax.fori_loop(0, (total + 7) // 8, body, 0)


def unfold(acc, rows):
    lane = lax.broadcasted_iota(jnp.int32, (rows, TILE), 1)
    total = None
    for j in range(8):
        line = acc[pl.ds(j, rows, stride=8), :]
        line = jnp.where(lane < 16, line + pltpu.roll(line, TILE - 16, 1), 0.0)
        line = pltpu.roll(line, 16 * j, 1) if j else line
        total = line if total is None else total + line
    return total


def fill_table(table, below, owned, above):
    count = owned.shape[0]
    for at, value in ((0, below), (RIM, owned), (RIM + count, above)):
        table[pl.ds(at, value.shape[0]), :] = value.astype(jnp.bfloat16).astype(jnp.float32)


def ascend_kernel(
    back, meta_ref, recv_ref, owned_ref, below_ref, above_ref,
    grad_ref, low_ref, high_ref, rounds_ref, words, base_of, slot_of, correl_ref,
    table, foot, starts, values, acc, from_row,
):
    groups = recv_ref.shape[0] // BLOCK
    rows = grad_ref.shape[0]
    fill_table(table, below_ref[...], owned_ref[...], above_ref[...])
    total, rounds = compact(meta_ref, groups, base_of, from_row, slot_of)
    rounds_ref[0, 0] = rounds
    rounds_ref[0, 1] = total
    fetch(total, recv_ref, from_row, words, table, base_of, foot)

    def give(here, weights, start, slope, correl):
        starts[here, :] = start
        for q in range(8):
            values[q, here, :] = weights[q] * slope
        if back:
            values[8, here, :] = correl

    sample(total, words, foot, give)
    if back:
        correl_ref[...] = jnp.zeros(correl_ref.shape, jnp.float32)
        send_back(total, values.at[8], slot_of, correl_ref)
    else:
        correl_ref[...] = jnp.zeros(correl_ref.shape, jnp.float32)
    splat_all(total, starts, values, base_of, acc)
    grad = unfold(acc, rows)
    grad_ref[...] = grad
    low_ref[...] = grad[: 2 * RIM]
    high_ref[...] = grad[rows - 2 * RIM :]


def forward_kernel(
    rounds_ref, base_of, slot_of, inside_ref, words, owned_ref, below_ref, above_ref, grad_ref, under_ref, over_ref,
    atlas_ref, slope_ref, correl_ref,
    table, foot, marks,
):
    own_rows = owned_ref.shape[0]
    rows = own_rows + 2 * RIM
    total = rounds_ref[0, 1]
    first = grad_ref[0 : 2 * RIM, :] + under_ref[...]
    last = grad_ref[rows - 2 * RIM : rows, :] + over_ref[...]
    below = (below_ref[...] + ascent * first[:RIM]) * inside_ref[0, 0]
    above = (above_ref[...] + ascent * last[RIM:]) * inside_ref[0, 1]
    atlas_ref[0:RIM, :] = owned_ref[0:RIM, :] + ascent * first[RIM:]
    atlas_ref[RIM : own_rows - RIM, :] = (
        owned_ref[RIM : own_rows - RIM, :] + ascent * grad_ref[2 * RIM : own_rows, :]
    )
    atlas_ref[own_rows - RIM : own_rows, :] = owned_ref[own_rows - RIM : own_rows, :] + ascent * last[:RIM]
    fill_table(table, below, atlas_ref[...], above)
    fetch(total, None, None, None, table, base_of, foot)

    def give(here, weights, start, slope, correl):
        slope_ref[here, :] = slope
        marks[here, :] = correl

    sample(total, words, foot, give)
    correl_ref[...] = jnp.zeros(correl_ref.shape, jnp.float32)
    send_back(total, marks, slot_of, correl_ref)


def backward_kernel(
    rounds_ref, base_of, words, slope_ref, atlas_ref, extra_ref,
    near_ref, low_ref, high_ref,
    starts, values, acc,
):
    own_rows = atlas_ref.shape[0]
    rows = own_rows + 2 * RIM
    total = rounds_ref[0, 1]

    def spread(step, carry):
        here = pl.ds(pl.multiple_of(step * STEP, STEP), STEP)
        second = words[1, here, :]
        slope = slope_ref[here, :]
        starts[here, :] = lax.shift_right_logical(second, 16)
        for q, weight in enumerate(weights_of(fractions_of(words[0, here, :], second))):
            values[q, here, :] = weight * slope
        return carry

    lax.fori_loop(0, (total + (STEP - 1)) // STEP, spread, 0)
    splat_all(total, starts, values, base_of, acc)
    grad = unfold(acc, rows) + extra_ref[...]
    low_ref[...] = grad[:RIM]
    high_ref[...] = grad[rows - RIM :]
    near_ref[...] = atlas_ref[...] + ascent * grad[RIM : RIM + own_rows]


def unpack_kernel(slot_ref, back_ref, extra_ref, correl_ref):
    slot = slot_ref[...]
    tiles = slot.shape[1]
    groups = back_ref.shape[0] // CAP
    total = jnp.zeros((PAD, tiles), jnp.float32)
    inner = lax.broadcasted_iota(jnp.int32, (PAD, tiles), 0)
    for g in range(groups):
        block = back_ref[pl.ds(g * CAP, CAP), :]
        block = jnp.concatenate([block, jnp.zeros((PAD - CAP, TILE), jnp.float32)], axis=0)
        wide = jnp.concatenate([block] * (tiles // TILE), axis=1)
        total = total + jnp.where(inner == slot - g * PAD, wide, 0.0)
    correl_ref[...] = jnp.sum(total, axis=0, keepdims=True) + extra_ref[...]


VMEM = pl.BlockSpec(memory_space=pltpu.VMEM)
SMEM = pl.BlockSpec(memory_space=pltpu.SMEM)
LIMIT = pltpu.CompilerParams(vmem_limit_bytes=48 * 1024 * 1024)


def shards(template, subject, tile_lists, corners, fractions, live_tiles):
    groups = lax.axis_size("subj")
    slabs = lax.axis_size("slab")
    owned = template[0]
    own_rows = owned.shape[0]
    tiles = subject.shape[2]
    rows = own_rows + 2 * RIM
    room = (groups * CAP + STEP) // STEP * STEP
    planes = jnp.transpose(fractions[0, 0], (1, 0, 2))
    f32, i32 = jnp.float32, jnp.int32

    def call(kernel, name, inputs, outputs, scratch=(), cost=3_000_000):
        return pl.pallas_call(
            kernel,
            out_shape=[jax.ShapeDtypeStruct(shape, kind) for shape, kind, _ in outputs],
            in_specs=[space for _, space in inputs],
            out_specs=[space for _, _, space in outputs],
            scratch_shapes=list(scratch),
            compiler_params=LIMIT,
            cost_estimate=pl.CostEstimate(flops=0, bytes_accessed=cost, transcendentals=0),
            name=name,
        )(*[value for value, _ in inputs])

    def pack(number):
        def kernel(*refs):
            pack_kernel(own_rows, *refs)

        return call(
            kernel,
            "pack",
            [(live_tiles, SMEM), (number, SMEM), (tile_lists[0, 0], VMEM), (corners[0, 0], VMEM), (planes, VMEM), (subject[0, 0], VMEM)],
            [((groups * BLOCK, TILE), i32, VMEM), ((1, tiles), i32, VMEM)],
        )

    def exchange(send):
        return lax.all_to_all(send, "subj", 0, 0, tiled=True)

    def ascend(recv, below, owned, above, back):
        meta = recv.reshape(groups, BLOCK, TILE)[:, META, :]

        def kernel(*refs):
            ascend_kernel(back, *refs)

        return call(
            kernel,
            "ascend",
            [(meta, SMEM), (recv, VMEM), (owned, VMEM), (below, VMEM), (above, VMEM)],
            [
                ((rows, TILE), f32, VMEM),
                ((2 * RIM, TILE), f32, VMEM),
                ((2 * RIM, TILE), f32, VMEM),
                ((1, 2), i32, SMEM),
                ((3, room, TILE), i32, VMEM),
                ((room,), i32, SMEM),
                ((room,), i32, SMEM),
                ((groups * CAP + 8 if back else 8, TILE), f32, VMEM),
            ],
            [
                pltpu.VMEM((rows, TILE), f32),
                pltpu.VMEM((SLOTS, room, TILE), f32),
                pltpu.VMEM((room, TILE), i32),
                pltpu.VMEM((9, room, TILE), f32),
                pltpu.VMEM((rows * 8, TILE), f32),
                pltpu.SMEM((room,), i32),
            ],
        )

    def unpack(slot, back, extra):
        return call(
            unpack_kernel,
            "unpack",
            [(slot, VMEM), (back, VMEM), (extra, VMEM)],
            [((1, tiles), f32, VMEM)],
        )[0]

    count = groups * slabs
    order = [(k % groups) * slabs + k // groups for k in range(count)]
    upward = [(order[k], order[k + 1]) for k in range(count - 1)]
    downward = [(order[k + 1], order[k]) for k in range(count - 1)]
    both = ("subj", "slab")
    place = lax.axis_index("slab") * groups + lax.axis_index("subj")
    inside = jnp.stack([place > 0, place < count - 1]).astype(f32).reshape(1, 2)

    def swap(low, high):
        return lax.ppermute(high, both, upward), lax.ppermute(low, both, downward)

    def later_rounds(rounds, state, work):
        def body(now):
            return (now[0] + 1, work(pack(now[0].reshape(1, 1)), now[1]))

        return lax.while_loop(lambda now: now[0] < rounds[0, 0], body, (jnp.int32(1), state))[1]

    below, above = swap(owned[:RIM], owned[own_rows - RIM :])
    send, slot = pack(jnp.zeros((1, 1), i32))
    recv = exchange(send)
    first = ascend(recv, below, owned, above, False)
    rounds, words, base_of, slot_of = first[3:7]

    def more_ascent(packed, state):
        found = ascend(exchange(packed[0]), below, owned, above, False)
        return tuple(now + term for now, term in zip(state, found[:3]))

    grad, low, high = later_rounds(rounds, tuple(first[:3]), more_ascent)
    under, over = swap(low, high)

    def last_round(packed, state):
        filler = jnp.zeros((rows - 4 * RIM, TILE), f32)
        atlas = jnp.concatenate([below, owned, above]) + ascent * (
            grad + jnp.concatenate([under, filler, over])
        )
        found = ascend(
            exchange(packed[0]),
            atlas[:RIM] * inside[0, 0],
            atlas[RIM : RIM + own_rows],
            atlas[RIM + own_rows :] * inside[0, 1],
            True,
        )
        back = exchange(found[7][: groups * CAP])
        return state[0] + found[0], unpack(packed[1], back, state[1])

    extra, extra_correl = later_rounds(
        rounds, (jnp.zeros((rows, TILE), f32), jnp.zeros((1, tiles), f32)), last_round
    )
    atlas, slope, correl_rows = call(
        forward_kernel,
        "forward",
        [
            (rounds, SMEM), (base_of, SMEM), (slot_of, SMEM), (inside, SMEM), (words, VMEM),
            (owned, VMEM), (below, VMEM), (above, VMEM), (grad, VMEM), (under, VMEM), (over, VMEM),
        ],
        [((own_rows, TILE), f32, VMEM), ((room, TILE), f32, VMEM), ((groups * CAP + 8, TILE), f32, VMEM)],
        [pltpu.VMEM((rows, TILE), f32), pltpu.VMEM((SLOTS, room, TILE), f32), pltpu.VMEM((room, TILE), f32)],
    )
    back = exchange(correl_rows[: groups * CAP])
    near, low, high = call(
        backward_kernel,
        "backward",
        [(rounds, SMEM), (base_of, SMEM), (words, VMEM), (slope, VMEM), (atlas, VMEM), (extra, VMEM)],
        [((own_rows, TILE), f32, VMEM), ((RIM, TILE), f32, VMEM), ((RIM, TILE), f32, VMEM)],
        [pltpu.VMEM((room, TILE), i32), pltpu.VMEM((8, room, TILE), f32), pltpu.VMEM((rows * 8, TILE), f32)],
    )
    under, over = swap(low, high)
    filler = jnp.zeros((own_rows - 2 * RIM, TILE), f32)
    current = near + ascent * jnp.concatenate([under, filler, over], axis=0)
    correl = unpack(slot, back, extra_correl)
    return (current[None], correl[None])


def solution(mesh):
    in_specs = (
        P("slab", "subj", None),
        P("subj", "slab", None, None),
        P("subj", "slab", None, None),
        P("subj", "slab", None, None, None),
        P("subj", "slab", None, None, None),
        P("subj", "slab"),
    )
    out_specs = (P("slab", "subj", None), P("subj", "slab", None))
    return jax.shard_map(shards, mesh=mesh, in_specs=in_specs, out_specs=out_specs, check_vma=False)
```

```python
import jax
import jax.numpy as jnp
from jax import lax
from jax.experimental import pallas as pl
from jax.experimental.pallas import tpu as pltpu
from jax.sharding import PartitionSpec as P

TILE = 128
SLOTS = 4
ROW = 8
ITERS = 2
HALO = 5
RIM = 8
CAP = 36
PAD = 40
META = 3 * CAP
BLOCK = 3 * CAP + 4
COUNT_AT = 126
MOST_AT = 127
FRAC_UNIT = 65535.0
U_UNIT = float(2**27)
STEP = 64
PART = 64
GROUP = 32

epsilon = 1e-05
ascent = 40.0

SPOTS = (0, 1, ROW, ROW + 1)
SHIFTS = (0, 1, 4, 5)


def pieces_of(word):
    return [
        ((word >> shift) & 255).astype(jnp.float32).astype(jnp.bfloat16) for shift in (0, 8, 16, 24)
    ]


def pack_kernel(own_rows, live_ref, round_ref, lists_ref, corners_ref, fractions_ref, subject_ref, send_ref, slot_ref):
    groups = send_ref.shape[0] // BLOCK
    tiles = subject_ref.shape[0]
    base = lists_ref[0:1, :]
    alive = lax.broadcasted_iota(jnp.int32, (1, tiles), 1) < live_ref[0, 0]
    owner = jnp.minimum(base // own_rows, groups - 1)
    local = base - owner * own_rows
    group_iota = lax.broadcasted_iota(jnp.int32, (groups, tiles), 0)
    member = jnp.where((group_iota == owner) & alive, 1.0, 0.0)
    before = lax.broadcasted_iota(jnp.int32, (tiles, tiles), 0) < lax.broadcasted_iota(
        jnp.int32, (tiles, tiles), 1
    )
    earlier = jnp.dot(
        member.astype(jnp.bfloat16),
        jnp.where(before, 1.0, 0.0).astype(jnp.bfloat16),
        preferred_element_type=jnp.float32,
    )
    counts = jnp.sum(member, axis=1, keepdims=True)
    first = round_ref[0, 0] * CAP
    rank = jnp.sum(member * earlier, axis=0, keepdims=True).astype(jnp.int32) - first
    chosen = alive & (rank >= 0) & (rank < CAP)
    slot = jnp.where(chosen, owner * PAD + rank, -1)
    slot_ref[...] = slot
    pick = jnp.where(
        lax.broadcasted_iota(jnp.int32, (groups * PAD, tiles), 0) == slot, 1.0, 0.0
    ).astype(jnp.bfloat16)

    at_rank = jnp.where(
        (lax.broadcasted_iota(jnp.int32, (TILE, tiles), 0) == rank) & chosen, 1.0, 0.0
    ).astype(jnp.bfloat16)
    local_high = (member * (local >> 4).astype(jnp.float32)).astype(jnp.bfloat16)
    local_low = (member * (local & 15).astype(jnp.float32)).astype(jnp.bfloat16)
    across = (((1,), (1,)), ((), ()))
    bases = 16.0 * lax.dot_general(
        local_high, at_rank, across, preferred_element_type=jnp.float32
    ) + lax.dot_general(local_low, at_rank, across, preferred_element_type=jnp.float32)
    here = jnp.clip(counts.astype(jnp.int32) - first, 0, CAP)
    most = jnp.max(counts, axis=0, keepdims=True).astype(jnp.int32)
    lane = lax.broadcasted_iota(jnp.int32, (groups, TILE), 1)
    header = jnp.where(
        lane == COUNT_AT, here, jnp.where(lane == MOST_AT, most, bases.astype(jnp.int32))
    )

    target = subject_ref[...].astype(jnp.float32)
    centered = target - jnp.mean(target, axis=-1, keepdims=True)
    subject_var = jnp.mean(centered * centered, axis=-1, keepdims=True) + epsilon
    unit = centered / jnp.sqrt(subject_var)
    coded = [
        (fractions_ref[d] * FRAC_UNIT + 0.5).astype(jnp.int32) for d in range(3)
    ]
    words = (
        coded[0] | (coded[1] << 16),
        coded[2] | (corners_ref[:, 0, :] << 16),
        jnp.round(unit * U_UNIT).astype(jnp.int32),
    )
    for w, word in enumerate(words):
        data = jnp.concatenate(pieces_of(word), axis=1)
        moved = jnp.dot(pick, data, preferred_element_type=jnp.float32)
        low = (moved[:, :TILE] + 256.0 * moved[:, TILE : 2 * TILE]).astype(jnp.int32)
        high = (moved[:, 2 * TILE : 3 * TILE] + 256.0 * moved[:, 3 * TILE :]).astype(jnp.int32)
        whole = low | (high << 16)
        for g in range(groups):
            send_ref[pl.ds(g * BLOCK + w * CAP, CAP), :] = whole[g * PAD : g * PAD + CAP]
    for g in range(groups):
        send_ref[pl.ds(g * BLOCK + META, 4), :] = jnp.broadcast_to(header[g : g + 1], (4, TILE))


def compact(meta_ref, groups, base_of, from_row, slot_of):
    def source(s, state):
        def take(r, place):
            base_of[place] = meta_ref[s, r] + (RIM - HALO)
            from_row[place] = s * BLOCK + r
            slot_of[place] = s * PAD + r
            return place + 1

        place = lax.fori_loop(0, meta_ref[s, COUNT_AT], take, state[0])
        return place, jnp.maximum(state[1], meta_ref[s, MOST_AT])

    total, most = lax.fori_loop(0, groups, source, (jnp.int32(0), jnp.int32(0)))
    for extra in range(GROUP):
        base_of[total + extra] = 0
        from_row[total + extra] = 0
        slot_of[total + extra] = PAD - 1
    return total, (most + (CAP - 1)) // CAP


def fetch(total, recv_ref, from_row, words, table, base_of, foot):
    def body(step, carry):
        at = pl.multiple_of(step * 8, 8)
        for i in range(8):
            here = pl.ds(at + i, 1)
            if recv_ref is not None:
                row = from_row[at + i]
                for w in range(3):
                    words[w, here, :] = recv_ref[pl.ds(row + w * CAP, 1), :]
            base = base_of[at + i]
            for k, shift in enumerate(SPOTS):
                foot[k, here, :] = table[pl.ds(base + shift, 1), :]
        return carry

    lax.fori_loop(0, (total + 7) // 8, body, 0)


def fractions_of(first, second):
    return (
        (first & 65535).astype(jnp.float32) * (1.0 / FRAC_UNIT),
        lax.shift_right_logical(first, 16).astype(jnp.float32) * (1.0 / FRAC_UNIT),
        (second & 65535).astype(jnp.float32) * (1.0 / FRAC_UNIT),
    )


def weights_of(along):
    away = [1.0 - x for x in along]
    found = []
    for q in range(8):
        weight = (
            (along[0] if q & 1 else away[0])
            * (along[1] if q & 2 else away[1])
            * (along[2] if q & 4 else away[2])
        )
        found.append(weight.astype(jnp.bfloat16).astype(jnp.float32))
    return found


def sample(total, words, foot, give):
    def piece(at):
        here = pl.ds(at, PART)
        second = words[1, here, :]
        unit = words[2, here, :].astype(jnp.float32) * (1.0 / U_UNIT)
        start = lax.shift_right_logical(second, 16)
        tables = [foot[k, here, :] for k in range(SLOTS)]
        weights = weights_of(fractions_of(words[0, here, :], second))
        warped = None
        for q in range(8):
            column = start + (SHIFTS[q & 3] + (16 if q & 4 else 0))
            lane = column & (TILE - 1)
            tile = column >> 7
            got = [
                jnp.take_along_axis(t, lane, axis=1, mode="promise_in_bounds", wrap_negative_indices=False) for t in tables
            ]
            picked = jnp.where(
                tile < 2, jnp.where(tile < 1, got[0], got[1]), jnp.where(tile < 3, got[2], got[3])
            )
            term = weights[q] * picked
            warped = term if warped is None else warped + term
        deviation = warped - jnp.mean(warped, axis=-1, keepdims=True)
        warp_var = jnp.mean(deviation * deviation, axis=-1, keepdims=True) + epsilon
        inverse = 1.0 / jnp.sqrt(warp_var)
        correl = jnp.mean(deviation * unit, axis=-1, keepdims=True) * inverse
        slope = (unit * inverse - (correl / warp_var) * deviation) * (1.0 / TILE)
        alive = at + lax.broadcasted_iota(jnp.int32, (PART, TILE), 0) < total
        slope = jnp.where(alive, slope, 0.0).astype(jnp.bfloat16).astype(jnp.float32)
        give(here, weights, start, slope, jnp.broadcast_to(correl, (PART, TILE)))

    def body(step, carry):
        for inner in range(0, STEP, PART):
            piece(pl.multiple_of(step * STEP + inner, PART))
        return carry

    lax.fori_loop(0, (total + (STEP - 1)) // STEP, body, 0)


def send_back(total, rows, slot_of, correl_ref):
    def body(step, carry):
        at = pl.multiple_of(step * 8, 8)
        for i in range(8):
            correl_ref[pl.ds(slot_of[at + i], 1), :] = rows[pl.ds(at + i, 1), :]
        return carry

    lax.fori_loop(0, (total + 7) // 8, body, 0)


def splat_all(total, starts, values, base_of, acc):
    acc[...] = jnp.zeros(acc.shape, jnp.float32)
    high_iota = lax.broadcasted_iota(jnp.int32, (32, TILE), 0)
    low_iota = lax.broadcasted_iota(jnp.int32, (16, TILE), 0)
    across = (((1,), (1,)), ((), ()))

    def body(step, carry):
        at = pl.multiple_of(step * GROUP, GROUP)
        for i in range(GROUP):
            line = pl.ds(at + i, 1)
            start = starts[line, :]
            high = (high_iota - (start >> 4)).astype(jnp.int16)
            low = (low_iota - (start & 15)).astype(jnp.int16)
            nothing = jnp.zeros((32, TILE), jnp.bfloat16)
            slope = jnp.broadcast_to(values[8, line, :], (32, TILE)).astype(jnp.bfloat16)
            sides = [jnp.where(high == jnp.int16(j), slope, nothing) for j in range(3)]
            corner = [
                jnp.broadcast_to(values[q, line, :], (16, TILE)).astype(jnp.bfloat16) for q in range(8)
            ]
            near, far = corner[:4], corner[4:]
            inside = [low == jnp.int16(shift) for shift in SHIFTS]
            wrapped = [low == jnp.int16(shift - 16) for shift in SHIFTS]
            parts = [nothing[:16] for _ in range(3)]
            for q in range(4):
                parts[0] = jnp.where(inside[q], near[q], parts[0])
                parts[1] = jnp.where(inside[q], far[q], parts[1])
                if q > 0:
                    parts[1] = jnp.where(wrapped[q], near[q], parts[1])
                    parts[2] = jnp.where(wrapped[q], far[q], parts[2])
            splat = lax.dot_general(
                jnp.concatenate(sides, axis=1),
                jnp.concatenate(parts, axis=1),
                across,
                preferred_element_type=jnp.float32,
            )
            base = base_of[at + i]
            spots = [pl.ds(pl.multiple_of((base + shift) * 8, 8), 8) for shift in SPOTS]
            sums = [acc[spots[k], 0:16] + splat[8 * k : 8 * k + 8] for k in range(SLOTS)]
            for k in range(SLOTS):
                acc[spots[k], 0:16] = sums[k]
        return carry

    lax.fori_loop(0, (total + (GROUP - 1)) // GROUP, body, 0)


def unfold(acc, rows):
    total = None
    for j in range(8):
        line = acc[pl.ds(j, rows, stride=8), :]
        line = pltpu.roll(line, 16 * j, 1) if j else line
        total = line if total is None else total + line
    return total


def fill_table(table, below, owned, above):
    count = owned.shape[0]
    for at, value in ((0, below), (RIM, owned), (RIM + count, above)):
        table[pl.ds(at, value.shape[0]), :] = value.astype(jnp.bfloat16).astype(jnp.float32)


def ascend_kernel(
    back, meta_ref, inside_ref, recv_ref, owned_ref, first_ref, second_ref,
    grad_ref, one_ref, two_ref, rounds_ref, words, base_of, slot_of, correl_ref,
    table, foot, starts, values, acc, from_row,
):
    groups = recv_ref.shape[0] // BLOCK
    rows = grad_ref.shape[0]
    odd = inside_ref[0, 2] > 0.0
    one, two = first_ref[...], second_ref[...]
    fill_table(table, jnp.where(odd, two, one), owned_ref[...], jnp.where(odd, one, two))
    total, rounds = compact(meta_ref, groups, base_of, from_row, slot_of)
    rounds_ref[0, 0] = rounds
    rounds_ref[0, 1] = total
    fetch(total, recv_ref, from_row, words, table, base_of, foot)

    def give(here, weights, start, slope, correl):
        starts[here, :] = start
        for q in range(8):
            values[q, here, :] = weights[q]
        values[8, here, :] = slope
        if back:
            values[9, here, :] = correl

    sample(total, words, foot, give)
    correl_ref[...] = jnp.zeros(correl_ref.shape, jnp.float32)
    if back:
        send_back(total, values.at[9], slot_of, correl_ref)
    splat_all(total, starts, values, base_of, acc)
    grad = unfold(acc, rows)
    grad_ref[...] = grad
    low, high = grad[: 2 * RIM], grad[rows - 2 * RIM :]
    one_ref[...] = jnp.where(odd, high, low)
    two_ref[...] = jnp.where(odd, low, high)


def forward_kernel(
    rounds_ref, base_of, slot_of, inside_ref, words, owned_ref, first_ref, second_ref, grad_ref, one_ref, two_ref,
    atlas_ref, slope_ref, correl_ref,
    table, foot, marks,
):
    own_rows = owned_ref.shape[0]
    rows = own_rows + 2 * RIM
    total = rounds_ref[0, 1]
    odd = inside_ref[0, 2] > 0.0
    one, two = one_ref[...], two_ref[...]
    first = grad_ref[0 : 2 * RIM, :] + jnp.where(odd, two, one)
    last = grad_ref[rows - 2 * RIM : rows, :] + jnp.where(odd, one, two)
    one, two = first_ref[...], second_ref[...]
    below = (jnp.where(odd, two, one) + ascent * first[:RIM]) * inside_ref[0, 0]
    above = (jnp.where(odd, one, two) + ascent * last[RIM:]) * inside_ref[0, 1]
    atlas_ref[0:RIM, :] = owned_ref[0:RIM, :] + ascent * first[RIM:]
    atlas_ref[RIM : own_rows - RIM, :] = (
        owned_ref[RIM : own_rows - RIM, :] + ascent * grad_ref[2 * RIM : own_rows, :]
    )
    atlas_ref[own_rows - RIM : own_rows, :] = owned_ref[own_rows - RIM : own_rows, :] + ascent * last[:RIM]
    fill_table(table, below, atlas_ref[...], above)
    fetch(total, None, None, None, table, base_of, foot)

    def give(here, weights, start, slope, correl):
        slope_ref[here, :] = slope
        marks[here, :] = correl

    sample(total, words, foot, give)
    correl_ref[...] = jnp.zeros(correl_ref.shape, jnp.float32)
    send_back(total, marks, slot_of, correl_ref)


def backward_kernel(
    rounds_ref, base_of, inside_ref, words, slope_ref, atlas_ref, extra_ref,
    near_ref, one_ref, two_ref,
    starts, values, acc,
):
    own_rows = atlas_ref.shape[0]
    rows = own_rows + 2 * RIM
    total = rounds_ref[0, 1]

    def spread(step, carry):
        here = pl.ds(pl.multiple_of(step * STEP, STEP), STEP)
        second = words[1, here, :]
        values[8, here, :] = slope_ref[here, :]
        starts[here, :] = lax.shift_right_logical(second, 16)
        for q, weight in enumerate(weights_of(fractions_of(words[0, here, :], second))):
            values[q, here, :] = weight
        return carry

    lax.fori_loop(0, (total + (STEP - 1)) // STEP, spread, 0)
    splat_all(total, starts, values, base_of, acc)
    grad = unfold(acc, rows) + extra_ref[...]
    odd = inside_ref[0, 2] > 0.0
    low, high = grad[:RIM], grad[rows - RIM :]
    one_ref[...] = jnp.where(odd, high, low)
    two_ref[...] = jnp.where(odd, low, high)
    near_ref[...] = atlas_ref[...] + ascent * grad[RIM : RIM + own_rows]


def unpack_kernel(slot_ref, back_ref, extra_ref, correl_ref):
    slot = slot_ref[...]
    tiles = slot.shape[1]
    total = jnp.zeros((PAD, tiles), jnp.float32)
    inner = lax.broadcasted_iota(jnp.int32, (PAD, tiles), 0)
    for g in range(back_ref.shape[0] // PAD):
        block = back_ref[pl.ds(g * PAD, PAD), :]
        wide = jnp.concatenate([block] * (tiles // TILE), axis=1)
        total = total + jnp.where(inner == slot - g * PAD, wide, 0.0)
    correl_ref[...] = jnp.sum(total, axis=0, keepdims=True) + extra_ref[...]


VMEM = pl.BlockSpec(memory_space=pltpu.VMEM)
SMEM = pl.BlockSpec(memory_space=pltpu.SMEM)
LIMIT = pltpu.CompilerParams(vmem_limit_bytes=48 * 1024 * 1024)


def shards(template, subject, tile_lists, corners, fractions, live_tiles):
    groups = lax.axis_size("subj")
    slabs = lax.axis_size("slab")
    owned = template[0]
    own_rows = owned.shape[0]
    tiles = subject.shape[2]
    rows = own_rows + 2 * RIM
    room = (groups * CAP + STEP) // STEP * STEP
    planes = jnp.transpose(fractions[0, 0], (1, 0, 2))
    f32, i32 = jnp.float32, jnp.int32

    def call(kernel, name, inputs, outputs, scratch=(), cost=3_000_000):
        return pl.pallas_call(
            kernel,
            out_shape=[jax.ShapeDtypeStruct(shape, kind) for shape, kind, _ in outputs],
            in_specs=[space for _, space in inputs],
            out_specs=[space for _, _, space in outputs],
            scratch_shapes=list(scratch),
            compiler_params=LIMIT,
            cost_estimate=pl.CostEstimate(flops=0, bytes_accessed=cost, transcendentals=0),
            name=name,
        )(*[value for value, _ in inputs])

    count = groups * slabs
    order = [(k % groups) * slabs + k // groups for k in range(count)]
    both = ("subj", "slab")
    place = lax.axis_index("slab") * groups + lax.axis_index("subj")
    odd = place % 2 == 1
    inside = jnp.stack([place > 0, place < count - 1, odd]).astype(f32).reshape(1, 3)

    def pairs_from(start):
        found = [(order[k], order[k + 1]) for k in range(start, count - 1, 2)]
        return found + [(there, here) for here, there in found]

    def swap(one, two):
        return lax.ppermute(one, both, pairs_from(1)), lax.ppermute(two, both, pairs_from(0))

    def sides(one, two):
        return jnp.where(odd, two, one), jnp.where(odd, one, two)

    def pack(number):
        def kernel(*refs):
            pack_kernel(own_rows, *refs)

        return call(
            kernel,
            "pack",
            [(live_tiles, SMEM), (number, SMEM), (tile_lists[0, 0], VMEM), (corners[0, 0], VMEM), (planes, VMEM), (subject[0, 0], VMEM)],
            [((groups * BLOCK, TILE), i32, VMEM), ((1, tiles), i32, VMEM)],
        )

    def exchange(send):
        return lax.all_to_all(send, "subj", 0, 0, tiled=True)

    def ascend(recv, one, owned, two, back):
        meta = recv.reshape(groups, BLOCK, TILE)[:, META, :]

        def kernel(*refs):
            ascend_kernel(back, *refs)

        return call(
            kernel,
            "ascend",
            [(meta, SMEM), (inside, SMEM), (recv, VMEM), (owned, VMEM), (one, VMEM), (two, VMEM)],
            [
                ((rows, TILE), f32, VMEM),
                ((2 * RIM, TILE), f32, VMEM),
                ((2 * RIM, TILE), f32, VMEM),
                ((1, 2), i32, SMEM),
                ((3, room, TILE), i32, VMEM),
                ((room,), i32, SMEM),
                ((room,), i32, SMEM),
                ((groups * PAD if back else 8, TILE), f32, VMEM),
            ],
            [
                pltpu.VMEM((rows, TILE), f32),
                pltpu.VMEM((SLOTS, room, TILE), f32),
                pltpu.VMEM((room, TILE), i32),
                pltpu.VMEM((10, room, TILE), f32),
                pltpu.VMEM((rows * 8, TILE), f32),
                pltpu.SMEM((room,), i32),
            ],
        )

    def unpack(slot, back, extra):
        return call(
            unpack_kernel,
            "unpack",
            [(slot, VMEM), (back, VMEM), (extra, VMEM)],
            [((1, tiles), f32, VMEM)],
        )[0]

    def later_rounds(rounds, state, work):
        def body(now):
            return (now[0] + 1, work(pack(now[0].reshape(1, 1)), now[1]))

        return lax.while_loop(lambda now: now[0] < rounds[0, 0], body, (jnp.int32(1), state))[1]

    low, high = owned[:RIM], owned[own_rows - RIM :]
    rims = swap(jnp.where(odd, high, low), jnp.where(odd, low, high))
    send, slot = pack(jnp.zeros((1, 1), i32))
    recv = exchange(send)
    first = ascend(recv, rims[0], owned, rims[1], False)
    rounds, words, base_of, slot_of = first[3:7]

    def more_ascent(packed, state):
        found = ascend(exchange(packed[0]), rims[0], owned, rims[1], False)
        return tuple(now + term for now, term in zip(state, found[:3]))

    grad, one, two = later_rounds(rounds, tuple(first[:3]), more_ascent)
    edges = swap(one, two)

    def last_round(packed, state):
        filler = jnp.zeros((rows - 4 * RIM, TILE), f32)
        below, above = sides(*rims)
        under, over = sides(*edges)
        atlas = jnp.concatenate([below, owned, above]) + ascent * (
            grad + jnp.concatenate([under, filler, over])
        )
        low = atlas[:RIM] * inside[0, 0]
        high = atlas[RIM + own_rows :] * inside[0, 1]
        one, two = sides(low, high)
        found = ascend(exchange(packed[0]), one, atlas[RIM : RIM + own_rows], two, True)
        return state[0] + found[0], unpack(packed[1], exchange(found[7]), state[1])

    extra, extra_correl = later_rounds(
        rounds, (jnp.zeros((rows, TILE), f32), jnp.zeros((1, tiles), f32)), last_round
    )
    atlas, slope, correl_rows = call(
        forward_kernel,
        "forward",
        [
            (rounds, SMEM), (base_of, SMEM), (slot_of, SMEM), (inside, SMEM), (words, VMEM),
            (owned, VMEM), (rims[0], VMEM), (rims[1], VMEM), (grad, VMEM), (edges[0], VMEM), (edges[1], VMEM),
        ],
        [((own_rows, TILE), f32, VMEM), ((room, TILE), f32, VMEM), ((groups * PAD, TILE), f32, VMEM)],
        [pltpu.VMEM((rows, TILE), f32), pltpu.VMEM((SLOTS, room, TILE), f32), pltpu.VMEM((room, TILE), f32)],
    )
    back = exchange(correl_rows)
    near, one, two = call(
        backward_kernel,
        "backward",
        [(rounds, SMEM), (base_of, SMEM), (inside, SMEM), (words, VMEM), (slope, VMEM), (atlas, VMEM), (extra, VMEM)],
        [((own_rows, TILE), f32, VMEM), ((RIM, TILE), f32, VMEM), ((RIM, TILE), f32, VMEM)],
        [pltpu.VMEM((room, TILE), i32), pltpu.VMEM((9, room, TILE), f32), pltpu.VMEM((rows * 8, TILE), f32)],
        30_000_000,
    )
    under, over = sides(*swap(one, two))
    filler = jnp.zeros((own_rows - 2 * RIM, TILE), f32)
    current = near + ascent * jnp.concatenate([under, filler, over], axis=0)
    correl = unpack(slot, back, extra_correl)
    return (current[None], correl[None])


def solution(mesh):
    in_specs = (
        P("slab", "subj", None),
        P("subj", "slab", None, None),
        P("subj", "slab", None, None),
        P("subj", "slab", None, None, None),
        P("subj", "slab", None, None, None),
        P("subj", "slab"),
    )
    out_specs = (P("slab", "subj", None), P("subj", "slab", None))
    return jax.shard_map(shards, mesh=mesh, in_specs=in_specs, out_specs=out_specs, check_vma=False)
```

```python
import jax
import jax.numpy as jnp
from jax import lax
from jax.experimental import pallas as pl
from jax.experimental.pallas import tpu as pltpu
from jax.sharding import PartitionSpec as P

TILE = 128
SLOTS = 4
ROW = 8
ITERS = 2
HALO = 5
RIM = 8
CAP = 36
PAD = 40
META = 3 * CAP
BLOCK = 3 * CAP + 4
COUNT_AT = 126
MOST_AT = 127
FRAC_UNIT = 65535.0
U_UNIT = float(2**27)
STEP = 64
PART = 64
GROUP = 32

epsilon = 1e-05
ascent = 40.0

SPOTS = (0, 1, ROW, ROW + 1)
SHIFTS = (0, 1, 4, 5)


def pieces_of(word):
    return [
        ((word >> shift) & 255).astype(jnp.float32).astype(jnp.bfloat16) for shift in (0, 8, 16, 24)
    ]


def pack_kernel(own_rows, live_ref, round_ref, lists_ref, corners_ref, fractions_ref, subject_ref, send_ref, slot_ref):
    groups = send_ref.shape[0] // BLOCK
    tiles = subject_ref.shape[0]
    base = lists_ref[0:1, :]
    alive = lax.broadcasted_iota(jnp.int32, (1, tiles), 1) < live_ref[0, 0]
    owner = jnp.minimum(base // own_rows, groups - 1)
    local = base - owner * own_rows
    group_iota = lax.broadcasted_iota(jnp.int32, (groups, tiles), 0)
    member = jnp.where((group_iota == owner) & alive, 1.0, 0.0)
    before = lax.broadcasted_iota(jnp.int32, (tiles, tiles), 0) < lax.broadcasted_iota(
        jnp.int32, (tiles, tiles), 1
    )
    earlier = jnp.dot(
        member.astype(jnp.bfloat16),
        jnp.where(before, 1.0, 0.0).astype(jnp.bfloat16),
        preferred_element_type=jnp.float32,
    )
    counts = jnp.sum(member, axis=1, keepdims=True)
    first = round_ref[0, 0] * CAP
    rank = jnp.sum(member * earlier, axis=0, keepdims=True).astype(jnp.int32) - first
    chosen = alive & (rank >= 0) & (rank < CAP)
    slot = jnp.where(chosen, owner * PAD + rank, -1)
    slot_ref[...] = slot
    pick = jnp.where(
        lax.broadcasted_iota(jnp.int32, (groups * PAD, tiles), 0) == slot, 1.0, 0.0
    ).astype(jnp.bfloat16)

    at_rank = jnp.where(
        (lax.broadcasted_iota(jnp.int32, (TILE, tiles), 0) == rank) & chosen, 1.0, 0.0
    ).astype(jnp.bfloat16)
    local_high = (member * (local >> 4).astype(jnp.float32)).astype(jnp.bfloat16)
    local_low = (member * (local & 15).astype(jnp.float32)).astype(jnp.bfloat16)
    across = (((1,), (1,)), ((), ()))
    bases = 16.0 * lax.dot_general(
        local_high, at_rank, across, preferred_element_type=jnp.float32
    ) + lax.dot_general(local_low, at_rank, across, preferred_element_type=jnp.float32)
    here = jnp.clip(counts.astype(jnp.int32) - first, 0, CAP)
    most = jnp.max(counts, axis=0, keepdims=True).astype(jnp.int32)
    lane = lax.broadcasted_iota(jnp.int32, (groups, TILE), 1)
    header = jnp.where(
        lane == COUNT_AT, here, jnp.where(lane == MOST_AT, most, bases.astype(jnp.int32))
    )

    target = subject_ref[...].astype(jnp.float32)
    centered = target - jnp.mean(target, axis=-1, keepdims=True)
    subject_var = jnp.mean(centered * centered, axis=-1, keepdims=True) + epsilon
    unit = centered / jnp.sqrt(subject_var)
    coded = [
        (fractions_ref[d] * FRAC_UNIT + 0.5).astype(jnp.int32) for d in range(3)
    ]
    words = (
        coded[0] | (coded[1] << 16),
        coded[2] | (corners_ref[:, 0, :] << 16),
        jnp.round(unit * U_UNIT).astype(jnp.int32),
    )
    for w, word in enumerate(words):
        data = jnp.concatenate(pieces_of(word), axis=1)
        moved = jnp.dot(pick, data, preferred_element_type=jnp.float32)
        low = (moved[:, :TILE] + 256.0 * moved[:, TILE : 2 * TILE]).astype(jnp.int32)
        high = (moved[:, 2 * TILE : 3 * TILE] + 256.0 * moved[:, 3 * TILE :]).astype(jnp.int32)
        whole = low | (high << 16)
        for g in range(groups):
            send_ref[pl.ds(g * BLOCK + w * CAP, CAP), :] = whole[g * PAD : g * PAD + CAP]
    for g in range(groups):
        send_ref[pl.ds(g * BLOCK + META, 4), :] = jnp.broadcast_to(header[g : g + 1], (4, TILE))


def compact(meta_ref, groups, base_of, from_row, slot_of):
    def source(s, state):
        def take(r, place):
            base_of[place] = meta_ref[s, r] + (RIM - HALO)
            from_row[place] = s * BLOCK + r
            slot_of[place] = s * PAD + r
            return place + 1

        place = lax.fori_loop(0, meta_ref[s, COUNT_AT], take, state[0])
        return place, jnp.maximum(state[1], meta_ref[s, MOST_AT])

    total, most = lax.fori_loop(0, groups, source, (jnp.int32(0), jnp.int32(0)))
    for extra in range(GROUP):
        base_of[total + extra] = 0
        from_row[total + extra] = 0
        slot_of[total + extra] = PAD - 1
    return total, (most + (CAP - 1)) // CAP


def fetch(total, recv_ref, from_row, words, table, base_of, foot):
    def body(step, carry):
        at = pl.multiple_of(step * 8, 8)
        for i in range(8):
            here = pl.ds(at + i, 1)
            if recv_ref is not None:
                row = from_row[at + i]
                for w in range(3):
                    words[w, here, :] = recv_ref[pl.ds(row + w * CAP, 1), :]
            base = base_of[at + i]
            for k, shift in enumerate(SPOTS):
                foot[k, here, :] = table[pl.ds(base + shift, 1), :]
        return carry

    lax.fori_loop(0, (total + 7) // 8, body, 0)


def fractions_of(first, second):
    return (
        (first & 65535).astype(jnp.float32) * (1.0 / FRAC_UNIT),
        lax.shift_right_logical(first, 16).astype(jnp.float32) * (1.0 / FRAC_UNIT),
        (second & 65535).astype(jnp.float32) * (1.0 / FRAC_UNIT),
    )


def weights_of(along):
    away = [1.0 - x for x in along]
    found = []
    for q in range(8):
        weight = (
            (along[0] if q & 1 else away[0])
            * (along[1] if q & 2 else away[1])
            * (along[2] if q & 4 else away[2])
        )
        found.append(weight.astype(jnp.bfloat16).astype(jnp.float32))
    return found


def sample(total, words, foot, give):
    def piece(at):
        here = pl.ds(at, PART)
        second = words[1, here, :]
        unit = words[2, here, :].astype(jnp.float32) * (1.0 / U_UNIT)
        start = lax.shift_right_logical(second, 16)
        tables = [foot[k, here, :] for k in range(SLOTS)]
        weights = weights_of(fractions_of(words[0, here, :], second))
        warped = None
        for q in range(8):
            column = start + (SHIFTS[q & 3] + (16 if q & 4 else 0))
            lane = column & (TILE - 1)
            tile = column >> 7
            got = [
                jnp.take_along_axis(t, lane, axis=1, mode="promise_in_bounds", wrap_negative_indices=False) for t in tables
            ]
            picked = jnp.where(
                tile < 2, jnp.where(tile < 1, got[0], got[1]), jnp.where(tile < 3, got[2], got[3])
            )
            term = weights[q] * picked
            warped = term if warped is None else warped + term
        deviation = warped - jnp.mean(warped, axis=-1, keepdims=True)
        warp_var = jnp.mean(deviation * deviation, axis=-1, keepdims=True) + epsilon
        inverse = 1.0 / jnp.sqrt(warp_var)
        correl = jnp.mean(deviation * unit, axis=-1, keepdims=True) * inverse
        slope = (unit * inverse - (correl / warp_var) * deviation) * (1.0 / TILE)
        alive = at + lax.broadcasted_iota(jnp.int32, (PART, TILE), 0) < total
        slope = jnp.where(alive, slope, 0.0).astype(jnp.bfloat16).astype(jnp.float32)
        give(here, weights, start, slope, jnp.broadcast_to(correl, (PART, TILE)))

    def body(step, carry):
        for inner in range(0, STEP, PART):
            piece(pl.multiple_of(step * STEP + inner, PART))
        return carry

    lax.fori_loop(0, (total + (STEP - 1)) // STEP, body, 0)


def send_back(total, rows, slot_of, correl_ref):
    def body(step, carry):
        at = pl.multiple_of(step * 8, 8)
        for i in range(8):
            correl_ref[pl.ds(slot_of[at + i], 1), :] = rows[pl.ds(at + i, 1), :]
        return carry

    lax.fori_loop(0, (total + 7) // 8, body, 0)


def splat_all(total, starts, values, base_of, acc):
    acc[...] = jnp.zeros(acc.shape, jnp.float32)
    high_iota = lax.broadcasted_iota(jnp.int32, (32, TILE), 0)
    low_iota = lax.broadcasted_iota(jnp.int32, (16, TILE), 0)
    across = (((1,), (1,)), ((), ()))

    def body(step, carry):
        at = pl.multiple_of(step * GROUP, GROUP)
        for i in range(GROUP):
            line = pl.ds(at + i, 1)
            start = starts[line, :]
            high = (high_iota - (start >> 4)).astype(jnp.int16)
            low = (low_iota - (start & 15)).astype(jnp.int16)
            nothing = jnp.zeros((32, TILE), jnp.bfloat16)
            slope = jnp.broadcast_to(values[8, line, :], (32, TILE)).astype(jnp.bfloat16)
            sides = [jnp.where(high == jnp.int16(j), slope, nothing) for j in range(3)]
            corner = [
                jnp.broadcast_to(values[q, line, :], (16, TILE)).astype(jnp.bfloat16) for q in range(8)
            ]
            near, far = corner[:4], corner[4:]
            inside = [low == jnp.int16(shift) for shift in SHIFTS]
            wrapped = [low == jnp.int16(shift - 16) for shift in SHIFTS]
            parts = [nothing[:16] for _ in range(3)]
            for q in range(4):
                parts[0] = jnp.where(inside[q], near[q], parts[0])
                parts[1] = jnp.where(inside[q], far[q], parts[1])
                if q > 0:
                    parts[1] = jnp.where(wrapped[q], near[q], parts[1])
                    parts[2] = jnp.where(wrapped[q], far[q], parts[2])
            splat = lax.dot_general(
                jnp.concatenate(sides, axis=1),
                jnp.concatenate(parts, axis=1),
                across,
                preferred_element_type=jnp.float32,
            )
            base = base_of[at + i]
            spots = [pl.ds(pl.multiple_of((base + shift) * 8, 8), 8) for shift in SPOTS]
            sums = [acc[spots[k], 0:16] + splat[8 * k : 8 * k + 8] for k in range(SLOTS)]
            for k in range(SLOTS):
                acc[spots[k], 0:16] = sums[k]
        return carry

    lax.fori_loop(0, (total + (GROUP - 1)) // GROUP, body, 0)


def unfold(acc, rows):
    total = None
    for j in range(8):
        line = acc[pl.ds(j, rows, stride=8), :]
        line = pltpu.roll(line, 16 * j, 1) if j else line
        total = line if total is None else total + line
    return total


def fill_table(table, below, owned, above):
    count = owned.shape[0]
    for at, value in ((0, below), (RIM, owned), (RIM + count, above)):
        table[pl.ds(at, value.shape[0]), :] = value.astype(jnp.bfloat16).astype(jnp.float32)


def ascend_kernel(
    back, meta_ref, inside_ref, recv_ref, owned_ref, first_ref, second_ref,
    grad_ref, one_ref, two_ref, rounds_ref, total_ref, words, base_of, slot_of, correl_ref,
    table, foot, starts, values, acc, from_row,
):
    groups = recv_ref.shape[0] // BLOCK
    rows = grad_ref.shape[0]
    odd = inside_ref[0, 2] > 0.0
    one, two = first_ref[...], second_ref[...]
    fill_table(table, jnp.where(odd, two, one), owned_ref[...], jnp.where(odd, one, two))
    total, rounds = compact(meta_ref, groups, base_of, from_row, slot_of)
    rounds_ref[0, 0] = rounds
    total_ref[0, 0] = total
    fetch(total, recv_ref, from_row, words, table, base_of, foot)

    def give(here, weights, start, slope, correl):
        starts[here, :] = start
        for q in range(8):
            values[q, here, :] = weights[q]
        values[8, here, :] = slope
        if back:
            values[9, here, :] = correl

    sample(total, words, foot, give)
    if back:
        send_back(total, values.at[9], slot_of, correl_ref)
    splat_all(total, starts, values, base_of, acc)
    grad = unfold(acc, rows)
    grad_ref[...] = grad
    low, high = grad[: 2 * RIM], grad[rows - 2 * RIM :]
    one_ref[...] = jnp.where(odd, high, low)
    two_ref[...] = jnp.where(odd, low, high)


def forward_kernel(
    total_ref, base_of, slot_of, inside_ref, words, owned_ref, first_ref, second_ref, grad_ref, one_ref, two_ref,
    atlas_ref, slope_ref, correl_ref,
    table, foot, marks,
):
    own_rows = owned_ref.shape[0]
    rows = own_rows + 2 * RIM
    total = total_ref[0, 0]
    odd = inside_ref[0, 2] > 0.0
    one, two = one_ref[...], two_ref[...]
    first = grad_ref[0 : 2 * RIM, :] + jnp.where(odd, two, one)
    last = grad_ref[rows - 2 * RIM : rows, :] + jnp.where(odd, one, two)
    one, two = first_ref[...], second_ref[...]
    below = (jnp.where(odd, two, one) + ascent * first[:RIM]) * inside_ref[0, 0]
    above = (jnp.where(odd, one, two) + ascent * last[RIM:]) * inside_ref[0, 1]
    atlas_ref[0:RIM, :] = owned_ref[0:RIM, :] + ascent * first[RIM:]
    atlas_ref[RIM : own_rows - RIM, :] = (
        owned_ref[RIM : own_rows - RIM, :] + ascent * grad_ref[2 * RIM : own_rows, :]
    )
    atlas_ref[own_rows - RIM : own_rows, :] = owned_ref[own_rows - RIM : own_rows, :] + ascent * last[:RIM]
    fill_table(table, below, atlas_ref[...], above)
    fetch(total, None, None, None, table, base_of, foot)

    def give(here, weights, start, slope, correl):
        slope_ref[here, :] = slope
        marks[here, :] = correl

    sample(total, words, foot, give)
    send_back(total, marks, slot_of, correl_ref)


def backward_kernel(
    total_ref, base_of, inside_ref, words, slope_ref, atlas_ref, extra_ref,
    near_ref, one_ref, two_ref,
    starts, values, acc,
):
    own_rows = atlas_ref.shape[0]
    rows = own_rows + 2 * RIM
    total = total_ref[0, 0]

    def spread(step, carry):
        here = pl.ds(pl.multiple_of(step * STEP, STEP), STEP)
        second = words[1, here, :]
        values[8, here, :] = slope_ref[here, :]
        starts[here, :] = lax.shift_right_logical(second, 16)
        for q, weight in enumerate(weights_of(fractions_of(words[0, here, :], second))):
            values[q, here, :] = weight
        return carry

    lax.fori_loop(0, (total + (STEP - 1)) // STEP, spread, 0)
    splat_all(total, starts, values, base_of, acc)
    grad = unfold(acc, rows) + extra_ref[...]
    odd = inside_ref[0, 2] > 0.0
    low, high = grad[:RIM], grad[rows - RIM :]
    one_ref[...] = jnp.where(odd, high, low)
    two_ref[...] = jnp.where(odd, low, high)
    near_ref[...] = atlas_ref[...] + ascent * grad[RIM : RIM + own_rows]


def finish_kernel(inside_ref, near_ref, one_ref, two_ref, atlas_ref):
    odd = inside_ref[0, 2] > 0.0
    one, two = one_ref[...], two_ref[...]
    atlas_ref[...] = near_ref[...]
    atlas_ref[0:RIM, :] += ascent * jnp.where(odd, two, one)
    rows = atlas_ref.shape[0]
    atlas_ref[rows - RIM : rows, :] += ascent * jnp.where(odd, one, two)


def unpack_kernel(slot_ref, back_ref, extra_ref, correl_ref):
    slot = slot_ref[...]
    tiles = slot.shape[1]
    total = jnp.zeros((PAD, tiles), jnp.float32)
    inner = lax.broadcasted_iota(jnp.int32, (PAD, tiles), 0)
    for g in range(back_ref.shape[0] // PAD):
        block = back_ref[pl.ds(g * PAD, PAD), :]
        wide = jnp.concatenate([block] * (tiles // TILE), axis=1)
        total = total + jnp.where(inner == slot - g * PAD, wide, 0.0)
    correl_ref[...] = jnp.sum(total, axis=0, keepdims=True) + extra_ref[...]


VMEM = pl.BlockSpec(memory_space=pltpu.VMEM)
SMEM = pl.BlockSpec(memory_space=pltpu.SMEM)
LIMIT = pltpu.CompilerParams(vmem_limit_bytes=48 * 1024 * 1024)


def shards(template, subject, tile_lists, corners, fractions, live_tiles):
    groups = lax.axis_size("subj")
    slabs = lax.axis_size("slab")
    owned = template[0]
    own_rows = owned.shape[0]
    tiles = subject.shape[2]
    rows = own_rows + 2 * RIM
    room = (groups * CAP + STEP) // STEP * STEP
    planes = jnp.transpose(fractions[0, 0], (1, 0, 2))
    f32, i32 = jnp.float32, jnp.int32

    def call(kernel, name, inputs, outputs, scratch=(), cost=3_000_000):
        return pl.pallas_call(
            kernel,
            out_shape=[jax.ShapeDtypeStruct(shape, kind) for shape, kind, _ in outputs],
            in_specs=[space for _, space in inputs],
            out_specs=[space for _, _, space in outputs],
            scratch_shapes=list(scratch),
            compiler_params=LIMIT,
            cost_estimate=pl.CostEstimate(flops=0, bytes_accessed=cost, transcendentals=0),
            name=name,
        )(*[value for value, _ in inputs])

    count = groups * slabs
    order = [(k % groups) * slabs + k // groups for k in range(count)]
    both = ("subj", "slab")
    place = lax.axis_index("slab") * groups + lax.axis_index("subj")
    odd = place % 2 == 1
    inside = jnp.stack([place > 0, place < count - 1, odd]).astype(f32).reshape(1, 3)

    def pairs_from(start):
        found = [(order[k], order[k + 1]) for k in range(start, count - 1, 2)]
        return found + [(there, here) for here, there in found]

    def swap(one, two):
        return lax.ppermute(one, both, pairs_from(1)), lax.ppermute(two, both, pairs_from(0))

    def sides(one, two):
        return jnp.where(odd, two, one), jnp.where(odd, one, two)

    def pack(number):
        def kernel(*refs):
            pack_kernel(own_rows, *refs)

        return call(
            kernel,
            "pack",
            [(live_tiles, SMEM), (number, SMEM), (tile_lists[0, 0], VMEM), (corners[0, 0], VMEM), (planes, VMEM), (subject[0, 0], VMEM)],
            [((groups * BLOCK, TILE), i32, VMEM), ((1, tiles), i32, VMEM)],
        )

    def exchange(send):
        return lax.all_to_all(send, "subj", 0, 0, tiled=True)

    def ascend(recv, one, owned, two, back):
        meta = recv.reshape(groups, BLOCK, TILE)[:, META, :]

        def kernel(*refs):
            ascend_kernel(back, *refs)

        return call(
            kernel,
            "ascend",
            [(meta, SMEM), (inside, SMEM), (recv, VMEM), (owned, VMEM), (one, VMEM), (two, VMEM)],
            [
                ((rows, TILE), f32, VMEM),
                ((2 * RIM, TILE), f32, VMEM),
                ((2 * RIM, TILE), f32, VMEM),
                ((1, 1), i32, SMEM),
                ((1, 1), i32, SMEM),
                ((3, room, TILE), i32, VMEM),
                ((room,), i32, SMEM),
                ((room,), i32, SMEM),
                ((groups * PAD if back else 8, TILE), f32, VMEM),
            ],
            [
                pltpu.VMEM((rows, TILE), f32),
                pltpu.VMEM((SLOTS, room, TILE), f32),
                pltpu.VMEM((room, TILE), i32),
                pltpu.VMEM((10, room, TILE), f32),
                pltpu.VMEM((rows * 8, TILE), f32),
                pltpu.SMEM((room,), i32),
            ],
        )

    def unpack(slot, back, extra):
        return call(
            unpack_kernel,
            "unpack",
            [(slot, VMEM), (back, VMEM), (extra, VMEM)],
            [((1, tiles), f32, VMEM)],
        )[0]

    def later_rounds(rounds, state, work):
        def body(now):
            return (now[0] + 1, work(pack(now[0].reshape(1, 1)), now[1]))

        return lax.while_loop(lambda now: now[0] < rounds[0, 0], body, (jnp.int32(1), state))[1]

    low, high = owned[:RIM], owned[own_rows - RIM :]
    rims = swap(jnp.where(odd, high, low), jnp.where(odd, low, high))
    send, slot = pack(jnp.zeros((1, 1), i32))
    recv = exchange(send)
    first = ascend(recv, rims[0], owned, rims[1], False)
    rounds, total, words, base_of, slot_of = first[3:8]

    def more_ascent(packed, state):
        found = ascend(exchange(packed[0]), rims[0], owned, rims[1], False)
        return tuple(now + term for now, term in zip(state, found[:3]))

    grad, one, two = later_rounds(rounds, tuple(first[:3]), more_ascent)
    edges = swap(one, two)

    def last_round(packed, state):
        filler = jnp.zeros((rows - 4 * RIM, TILE), f32)
        below, above = sides(*rims)
        under, over = sides(*edges)
        atlas = jnp.concatenate([below, owned, above]) + ascent * (
            grad + jnp.concatenate([under, filler, over])
        )
        low = atlas[:RIM] * inside[0, 0]
        high = atlas[RIM + own_rows :] * inside[0, 1]
        one, two = sides(low, high)
        found = ascend(exchange(packed[0]), one, atlas[RIM : RIM + own_rows], two, True)
        return state[0] + found[0], unpack(packed[1], exchange(found[8]), state[1])

    extra, extra_correl = later_rounds(
        rounds, (jnp.zeros((rows, TILE), f32), jnp.zeros((1, tiles), f32)), last_round
    )
    atlas, slope, correl_rows = call(
        forward_kernel,
        "forward",
        [
            (total, SMEM), (base_of, SMEM), (slot_of, SMEM), (inside, SMEM), (words, VMEM),
            (owned, VMEM), (rims[0], VMEM), (rims[1], VMEM), (grad, VMEM), (edges[0], VMEM), (edges[1], VMEM),
        ],
        [((own_rows, TILE), f32, VMEM), ((room, TILE), f32, VMEM), ((groups * PAD, TILE), f32, VMEM)],
        [pltpu.VMEM((rows, TILE), f32), pltpu.VMEM((SLOTS, room, TILE), f32), pltpu.VMEM((room, TILE), f32)],
    )
    back = exchange(correl_rows)
    near, one, two = call(
        backward_kernel,
        "backward",
        [(total, SMEM), (base_of, SMEM), (inside, SMEM), (words, VMEM), (slope, VMEM), (atlas, VMEM), (extra, VMEM)],
        [((own_rows, TILE), f32, VMEM), ((RIM, TILE), f32, VMEM), ((RIM, TILE), f32, VMEM)],
        [pltpu.VMEM((room, TILE), i32), pltpu.VMEM((9, room, TILE), f32), pltpu.VMEM((rows * 8, TILE), f32)],
        30_000_000,
    )
    last = swap(one, two)
    current = call(
        finish_kernel,
        "finish",
        [(inside, SMEM), (near, VMEM), (last[0], VMEM), (last[1], VMEM)],
        [((own_rows, TILE), f32, VMEM)],
        (),
        100_000,
    )[0]
    correl = unpack(slot, back, extra_correl)
    return (current[None], correl[None])


def solution(mesh):
    in_specs = (
        P("slab", "subj", None),
        P("subj", "slab", None, None),
        P("subj", "slab", None, None),
        P("subj", "slab", None, None, None),
        P("subj", "slab", None, None, None),
        P("subj", "slab"),
    )
    out_specs = (P("slab", "subj", None), P("subj", "slab", None))
    return jax.shard_map(shards, mesh=mesh, in_specs=in_specs, out_specs=out_specs, check_vma=False)
```

```python
import jax
import jax.numpy as jnp
from jax import lax
from jax.experimental import pallas as pl
from jax.experimental.pallas import tpu as pltpu
from jax.sharding import PartitionSpec as P

TILE = 128
SLOTS = 4
ROW = 8
ITERS = 2
HALO = 5
RIM = 8
CAP = 36
PAD = 40
META = 3 * CAP
BLOCK = 3 * CAP + 4
COUNT_AT = 126
MOST_AT = 127
FRAC_UNIT = 65535.0
U_UNIT = float(2**27)
STEP = 64
PART = 64
GROUP = 32

epsilon = 1e-05
ascent = 40.0

SPOTS = (0, 1, ROW, ROW + 1)
SHIFTS = (0, 1, 4, 5)


def pieces_of(word):
    return [
        ((word >> shift) & 255).astype(jnp.float32).astype(jnp.bfloat16) for shift in (0, 8, 16, 24)
    ]


def pack_kernel(own_rows, live_ref, round_ref, lists_ref, corners_ref, fractions_ref, subject_ref, send_ref, slot_ref):
    groups = send_ref.shape[0] // BLOCK
    tiles = subject_ref.shape[0]
    base = lists_ref[0:1, :]
    alive = lax.broadcasted_iota(jnp.int32, (1, tiles), 1) < live_ref[0, 0]
    owner = jnp.minimum(base // own_rows, groups - 1)
    local = base - owner * own_rows
    group_iota = lax.broadcasted_iota(jnp.int32, (groups, tiles), 0)
    member = jnp.where((group_iota == owner) & alive, 1.0, 0.0)
    before = lax.broadcasted_iota(jnp.int32, (tiles, tiles), 0) < lax.broadcasted_iota(
        jnp.int32, (tiles, tiles), 1
    )
    earlier = jnp.dot(
        member.astype(jnp.bfloat16),
        jnp.where(before, 1.0, 0.0).astype(jnp.bfloat16),
        preferred_element_type=jnp.float32,
    )
    counts = jnp.sum(member, axis=1, keepdims=True)
    first = round_ref[0, 0] * CAP
    rank = jnp.sum(member * earlier, axis=0, keepdims=True).astype(jnp.int32) - first
    chosen = alive & (rank >= 0) & (rank < CAP)
    slot = jnp.where(chosen, owner * PAD + rank, -1)
    slot_ref[...] = slot
    pick = jnp.where(
        lax.broadcasted_iota(jnp.int32, (groups * PAD, tiles), 0) == slot, 1.0, 0.0
    ).astype(jnp.bfloat16)

    at_rank = jnp.where(
        (lax.broadcasted_iota(jnp.int32, (TILE, tiles), 0) == rank) & chosen, 1.0, 0.0
    ).astype(jnp.bfloat16)
    local_high = (member * (local >> 4).astype(jnp.float32)).astype(jnp.bfloat16)
    local_low = (member * (local & 15).astype(jnp.float32)).astype(jnp.bfloat16)
    across = (((1,), (1,)), ((), ()))
    bases = 16.0 * lax.dot_general(
        local_high, at_rank, across, preferred_element_type=jnp.float32
    ) + lax.dot_general(local_low, at_rank, across, preferred_element_type=jnp.float32)
    here = jnp.clip(counts.astype(jnp.int32) - first, 0, CAP)
    most = jnp.max(counts, axis=0, keepdims=True).astype(jnp.int32)
    lane = lax.broadcasted_iota(jnp.int32, (groups, TILE), 1)
    header = jnp.where(
        lane == COUNT_AT, here, jnp.where(lane == MOST_AT, most, bases.astype(jnp.int32))
    )

    target = subject_ref[...].astype(jnp.float32)
    centered = target - jnp.mean(target, axis=-1, keepdims=True)
    subject_var = jnp.mean(centered * centered, axis=-1, keepdims=True) + epsilon
    unit = centered / jnp.sqrt(subject_var)
    coded = [
        (fractions_ref[d] * FRAC_UNIT + 0.5).astype(jnp.int32) for d in range(3)
    ]
    words = (
        coded[0] | (coded[1] << 16),
        coded[2] | (corners_ref[:, 0, :] << 16),
        jnp.round(unit * U_UNIT).astype(jnp.int32),
    )
    for w, word in enumerate(words):
        data = jnp.concatenate(pieces_of(word), axis=1)
        moved = jnp.dot(pick, data, preferred_element_type=jnp.float32)
        low = (moved[:, :TILE] + 256.0 * moved[:, TILE : 2 * TILE]).astype(jnp.int32)
        high = (moved[:, 2 * TILE : 3 * TILE] + 256.0 * moved[:, 3 * TILE :]).astype(jnp.int32)
        whole = low | (high << 16)
        for g in range(groups):
            send_ref[pl.ds(g * BLOCK + w * CAP, CAP), :] = whole[g * PAD : g * PAD + CAP]
    for g in range(groups):
        send_ref[pl.ds(g * BLOCK + META, 4), :] = jnp.broadcast_to(header[g : g + 1], (4, TILE))


def compact(meta_ref, groups, base_of, from_row, slot_of):
    def source(s, state):
        def take(r, place):
            base_of[place] = meta_ref[s, r] + (RIM - HALO)
            from_row[place] = s * BLOCK + r
            slot_of[place] = s * PAD + r
            return place + 1

        place = lax.fori_loop(0, meta_ref[s, COUNT_AT], take, state[0])
        return place, jnp.maximum(state[1], meta_ref[s, MOST_AT])

    total, most = lax.fori_loop(0, groups, source, (jnp.int32(0), jnp.int32(0)))
    for extra in range(GROUP):
        base_of[total + extra] = 0
        from_row[total + extra] = 0
        slot_of[total + extra] = PAD - 1
    return total, (most + (CAP - 1)) // CAP


def fetch(total, recv_ref, from_row, words, table, base_of, foot):
    def body(step, carry):
        at = pl.multiple_of(step * 8, 8)
        for i in range(8):
            here = pl.ds(at + i, 1)
            if recv_ref is not None:
                row = from_row[at + i]
                for w in range(3):
                    words[w, here, :] = recv_ref[pl.ds(row + w * CAP, 1), :]
            base = base_of[at + i]
            for k, shift in enumerate(SPOTS):
                foot[k, here, :] = table[pl.ds(base + shift, 1), :]
        return carry

    lax.fori_loop(0, (total + 7) // 8, body, 0)


def fractions_of(first, second):
    return (
        (first & 65535).astype(jnp.float32) * (1.0 / FRAC_UNIT),
        lax.shift_right_logical(first, 16).astype(jnp.float32) * (1.0 / FRAC_UNIT),
        (second & 65535).astype(jnp.float32) * (1.0 / FRAC_UNIT),
    )


def weights_of(along):
    away = [1.0 - x for x in along]
    found = []
    for q in range(8):
        weight = (
            (along[0] if q & 1 else away[0])
            * (along[1] if q & 2 else away[1])
            * (along[2] if q & 4 else away[2])
        )
        found.append(weight.astype(jnp.bfloat16).astype(jnp.float32))
    return found


def sample(total, words, foot, give):
    def piece(at):
        here = pl.ds(at, PART)
        second = words[1, here, :]
        unit = words[2, here, :].astype(jnp.float32) * (1.0 / U_UNIT)
        start = lax.shift_right_logical(second, 16)
        tables = [foot[k, here, :] for k in range(SLOTS)]
        weights = weights_of(fractions_of(words[0, here, :], second))
        peak = jnp.abs(tables[0])
        for t in tables[1:]:
            peak = jnp.maximum(peak, jnp.abs(t))
        peak = jnp.max(peak, axis=-1, keepdims=True)
        scale = jnp.where(peak > 0.0, 32767.0 / peak, 0.0)
        codes = [jnp.round(t * scale).astype(jnp.int32) for t in tables]
        couples = [(codes[k] & 65535) | (codes[k + 1] << 16) for k in (0, 2)]
        warped = None
        for q in range(8):
            column = start + (SHIFTS[q & 3] + (16 if q & 4 else 0))
            lane = column & (TILE - 1)
            got = [
                jnp.take_along_axis(c, lane, axis=1, mode="promise_in_bounds", wrap_negative_indices=False)
                for c in couples
            ]
            word = jnp.where(column < 2 * TILE, got[0], got[1])
            word = lax.shift_left(word, 16 - ((column >> 3) & 16))
            picked = lax.shift_right_arithmetic(word, jnp.full_like(word, 16)).astype(jnp.float32)
            term = weights[q] * picked
            warped = term if warped is None else warped + term
        warped = warped * (peak * (1.0 / 32767.0))
        deviation = warped - jnp.mean(warped, axis=-1, keepdims=True)
        warp_var = jnp.mean(deviation * deviation, axis=-1, keepdims=True) + epsilon
        inverse = 1.0 / jnp.sqrt(warp_var)
        correl = jnp.mean(deviation * unit, axis=-1, keepdims=True) * inverse
        slope = (unit * inverse - (correl / warp_var) * deviation) * (1.0 / TILE)
        alive = at + lax.broadcasted_iota(jnp.int32, (PART, TILE), 0) < total
        slope = jnp.where(alive, slope, 0.0).astype(jnp.bfloat16).astype(jnp.float32)
        give(here, weights, start, slope, jnp.broadcast_to(correl, (PART, TILE)))

    def body(step, carry):
        for inner in range(0, STEP, PART):
            piece(pl.multiple_of(step * STEP + inner, PART))
        return carry

    lax.fori_loop(0, (total + (STEP - 1)) // STEP, body, 0)


def send_back(total, rows, slot_of, correl_ref):
    def body(step, carry):
        at = pl.multiple_of(step * 8, 8)
        for i in range(8):
            correl_ref[pl.ds(slot_of[at + i], 1), :] = rows[pl.ds(at + i, 1), :]
        return carry

    lax.fori_loop(0, (total + 7) // 8, body, 0)


def splat_all(total, starts, values, base_of, acc):
    acc[...] = jnp.zeros(acc.shape, jnp.float32)
    high_iota = lax.broadcasted_iota(jnp.int32, (32, TILE), 0)
    low_iota = lax.broadcasted_iota(jnp.int32, (16, TILE), 0)
    across = (((1,), (1,)), ((), ()))

    def body(step, carry):
        at = pl.multiple_of(step * GROUP, GROUP)
        for i in range(GROUP):
            line = pl.ds(at + i, 1)
            start = starts[line, :]
            high = (high_iota - (start >> 4)).astype(jnp.int16)
            low = (low_iota - (start & 15)).astype(jnp.int16)
            nothing = jnp.zeros((32, TILE), jnp.bfloat16)
            slope = jnp.broadcast_to(values[8, line, :], (32, TILE)).astype(jnp.bfloat16)
            sides = [jnp.where(high == jnp.int16(j), slope, nothing) for j in range(3)]
            corner = [
                jnp.broadcast_to(values[q, line, :], (16, TILE)).astype(jnp.bfloat16) for q in range(8)
            ]
            near, far = corner[:4], corner[4:]
            inside = [low == jnp.int16(shift) for shift in SHIFTS]
            wrapped = [low == jnp.int16(shift - 16) for shift in SHIFTS]
            parts = [nothing[:16] for _ in range(3)]
            for q in range(4):
                parts[0] = jnp.where(inside[q], near[q], parts[0])
                parts[1] = jnp.where(inside[q], far[q], parts[1])
                if q > 0:
                    parts[1] = jnp.where(wrapped[q], near[q], parts[1])
                    parts[2] = jnp.where(wrapped[q], far[q], parts[2])
            splat = lax.dot_general(
                jnp.concatenate(sides, axis=1),
                jnp.concatenate(parts, axis=1),
                across,
                preferred_element_type=jnp.float32,
            )
            base = base_of[at + i]
            spots = [pl.ds(pl.multiple_of((base + shift) * 8, 8), 8) for shift in SPOTS]
            sums = [acc[spots[k], 0:16] + splat[8 * k : 8 * k + 8] for k in range(SLOTS)]
            for k in range(SLOTS):
                acc[spots[k], 0:16] = sums[k]
        return carry

    lax.fori_loop(0, (total + (GROUP - 1)) // GROUP, body, 0)


def unfold(acc, rows):
    total = None
    for j in range(8):
        line = acc[pl.ds(j, rows, stride=8), :]
        line = pltpu.roll(line, 16 * j, 1) if j else line
        total = line if total is None else total + line
    return total


def fill_table(table, below, owned, above):
    count = owned.shape[0]
    for at, value in ((0, below), (RIM, owned), (RIM + count, above)):
        table[pl.ds(at, value.shape[0]), :] = value.astype(jnp.bfloat16).astype(jnp.float32)


def ascend_kernel(
    back, meta_ref, inside_ref, recv_ref, owned_ref, first_ref, second_ref,
    grad_ref, one_ref, two_ref, rounds_ref, total_ref, words, base_of, slot_of, correl_ref,
    table, foot, starts, values, acc, from_row,
):
    groups = recv_ref.shape[0] // BLOCK
    rows = grad_ref.shape[0]
    odd = inside_ref[0, 2] > 0.0
    one, two = first_ref[...], second_ref[...]
    fill_table(table, jnp.where(odd, two, one), owned_ref[...], jnp.where(odd, one, two))
    total, rounds = compact(meta_ref, groups, base_of, from_row, slot_of)
    rounds_ref[0, 0] = rounds
    total_ref[0, 0] = total
    fetch(total, recv_ref, from_row, words, table, base_of, foot)

    def give(here, weights, start, slope, correl):
        starts[here, :] = start
        for q in range(8):
            values[q, here, :] = weights[q]
        values[8, here, :] = slope
        if back:
            values[9, here, :] = correl

    sample(total, words, foot, give)
    if back:
        send_back(total, values.at[9], slot_of, correl_ref)
    splat_all(total, starts, values, base_of, acc)
    grad = unfold(acc, rows)
    grad_ref[...] = grad
    low, high = grad[: 2 * RIM], grad[rows - 2 * RIM :]
    one_ref[...] = jnp.where(odd, high, low)
    two_ref[...] = jnp.where(odd, low, high)


def forward_kernel(
    total_ref, base_of, slot_of, inside_ref, words, owned_ref, first_ref, second_ref, grad_ref, one_ref, two_ref,
    atlas_ref, slope_ref, correl_ref,
    table, foot, marks,
):
    own_rows = owned_ref.shape[0]
    rows = own_rows + 2 * RIM
    total = total_ref[0, 0]
    odd = inside_ref[0, 2] > 0.0
    one, two = one_ref[...], two_ref[...]
    first = grad_ref[0 : 2 * RIM, :] + jnp.where(odd, two, one)
    last = grad_ref[rows - 2 * RIM : rows, :] + jnp.where(odd, one, two)
    one, two = first_ref[...], second_ref[...]
    below = (jnp.where(odd, two, one) + ascent * first[:RIM]) * inside_ref[0, 0]
    above = (jnp.where(odd, one, two) + ascent * last[RIM:]) * inside_ref[0, 1]
    atlas_ref[0:RIM, :] = owned_ref[0:RIM, :] + ascent * first[RIM:]
    atlas_ref[RIM : own_rows - RIM, :] = (
        owned_ref[RIM : own_rows - RIM, :] + ascent * grad_ref[2 * RIM : own_rows, :]
    )
    atlas_ref[own_rows - RIM : own_rows, :] = owned_ref[own_rows - RIM : own_rows, :] + ascent * last[:RIM]
    fill_table(table, below, atlas_ref[...], above)
    fetch(total, None, None, None, table, base_of, foot)

    def give(here, weights, start, slope, correl):
        slope_ref[here, :] = slope
        marks[here, :] = correl

    sample(total, words, foot, give)
    send_back(total, marks, slot_of, correl_ref)


def backward_kernel(
    total_ref, base_of, inside_ref, words, slope_ref, atlas_ref, extra_ref,
    near_ref, one_ref, two_ref,
    starts, values, acc,
):
    own_rows = atlas_ref.shape[0]
    rows = own_rows + 2 * RIM
    total = total_ref[0, 0]

    def spread(step, carry):
        here = pl.ds(pl.multiple_of(step * STEP, STEP), STEP)
        second = words[1, here, :]
        values[8, here, :] = slope_ref[here, :]
        starts[here, :] = lax.shift_right_logical(second, 16)
        for q, weight in enumerate(weights_of(fractions_of(words[0, here, :], second))):
            values[q, here, :] = weight
        return carry

    lax.fori_loop(0, (total + (STEP - 1)) // STEP, spread, 0)
    splat_all(total, starts, values, base_of, acc)
    grad = unfold(acc, rows) + extra_ref[...]
    odd = inside_ref[0, 2] > 0.0
    low, high = grad[:RIM], grad[rows - RIM :]
    one_ref[...] = jnp.where(odd, high, low)
    two_ref[...] = jnp.where(odd, low, high)
    near_ref[...] = atlas_ref[...] + ascent * grad[RIM : RIM + own_rows]


def unpack_kernel(slot_ref, back_ref, extra_ref, correl_ref):
    slot = slot_ref[...]
    tiles = slot.shape[1]
    total = jnp.zeros((PAD, tiles), jnp.float32)
    inner = lax.broadcasted_iota(jnp.int32, (PAD, tiles), 0)
    for g in range(back_ref.shape[0] // PAD):
        block = back_ref[pl.ds(g * PAD, PAD), :]
        wide = jnp.concatenate([block] * (tiles // TILE), axis=1)
        total = total + jnp.where(inner == slot - g * PAD, wide, 0.0)
    correl_ref[...] = jnp.sum(total, axis=0, keepdims=True) + extra_ref[...]


def finish_kernel(
    inside_ref, near_ref, one_ref, two_ref, slot_ref, back_ref, extra_ref, atlas_ref, correl_ref
):
    odd = inside_ref[0, 2] > 0.0
    one, two = one_ref[...], two_ref[...]
    atlas_ref[...] = near_ref[...]
    atlas_ref[0:RIM, :] += ascent * jnp.where(odd, two, one)
    rows = atlas_ref.shape[0]
    atlas_ref[rows - RIM : rows, :] += ascent * jnp.where(odd, one, two)
    unpack_kernel(slot_ref, back_ref, extra_ref, correl_ref)


VMEM = pl.BlockSpec(memory_space=pltpu.VMEM)
SMEM = pl.BlockSpec(memory_space=pltpu.SMEM)
LIMIT = pltpu.CompilerParams(vmem_limit_bytes=48 * 1024 * 1024)


def shards(template, subject, tile_lists, corners, fractions, live_tiles):
    groups = lax.axis_size("subj")
    slabs = lax.axis_size("slab")
    owned = template[0]
    own_rows = owned.shape[0]
    tiles = subject.shape[2]
    rows = own_rows + 2 * RIM
    room = (groups * CAP + STEP) // STEP * STEP
    planes = jnp.transpose(fractions[0, 0], (1, 0, 2))
    f32, i32 = jnp.float32, jnp.int32

    def call(kernel, name, inputs, outputs, scratch=(), cost=3_000_000):
        return pl.pallas_call(
            kernel,
            out_shape=[jax.ShapeDtypeStruct(shape, kind) for shape, kind, _ in outputs],
            in_specs=[space for _, space in inputs],
            out_specs=[space for _, _, space in outputs],
            scratch_shapes=list(scratch),
            compiler_params=LIMIT,
            cost_estimate=pl.CostEstimate(flops=0, bytes_accessed=cost, transcendentals=0),
            name=name,
        )(*[value for value, _ in inputs])

    count = groups * slabs
    order = [(k % groups) * slabs + k // groups for k in range(count)]
    both = ("subj", "slab")
    place = lax.axis_index("slab") * groups + lax.axis_index("subj")
    odd = place % 2 == 1
    inside = jnp.stack([place > 0, place < count - 1, odd]).astype(f32).reshape(1, 3)

    def pairs_from(start):
        found = [(order[k], order[k + 1]) for k in range(start, count - 1, 2)]
        return found + [(there, here) for here, there in found]

    def swap(one, two):
        return lax.ppermute(one, both, pairs_from(1)), lax.ppermute(two, both, pairs_from(0))

    def sides(one, two):
        return jnp.where(odd, two, one), jnp.where(odd, one, two)

    def pack(number):
        def kernel(*refs):
            pack_kernel(own_rows, *refs)

        return call(
            kernel,
            "pack",
            [(live_tiles, SMEM), (number, SMEM), (tile_lists[0, 0], VMEM), (corners[0, 0], VMEM), (planes, VMEM), (subject[0, 0], VMEM)],
            [((groups * BLOCK, TILE), i32, VMEM), ((1, tiles), i32, VMEM)],
        )

    def exchange(send):
        return lax.all_to_all(send, "subj", 0, 0, tiled=True)

    def ascend(recv, one, owned, two, back):
        meta = recv.reshape(groups, BLOCK, TILE)[:, META, :]

        def kernel(*refs):
            ascend_kernel(back, *refs)

        return call(
            kernel,
            "ascend",
            [(meta, SMEM), (inside, SMEM), (recv, VMEM), (owned, VMEM), (one, VMEM), (two, VMEM)],
            [
                ((rows, TILE), f32, VMEM),
                ((2 * RIM, TILE), f32, VMEM),
                ((2 * RIM, TILE), f32, VMEM),
                ((1, 1), i32, SMEM),
                ((1, 1), i32, SMEM),
                ((3, room, TILE), i32, VMEM),
                ((room,), i32, SMEM),
                ((room,), i32, SMEM),
                ((groups * PAD if back else 8, TILE), f32, VMEM),
            ],
            [
                pltpu.VMEM((rows, TILE), f32),
                pltpu.VMEM((SLOTS, room, TILE), f32),
                pltpu.VMEM((room, TILE), i32),
                pltpu.VMEM((10, room, TILE), f32),
                pltpu.VMEM((rows * 8, TILE), f32),
                pltpu.SMEM((room,), i32),
            ],
        )

    def unpack(slot, back, extra):
        return call(
            unpack_kernel,
            "unpack",
            [(slot, VMEM), (back, VMEM), (extra, VMEM)],
            [((1, tiles), f32, VMEM)],
        )[0]

    def later_rounds(rounds, state, work):
        def body(now):
            return (now[0] + 1, work(pack(now[0].reshape(1, 1)), now[1]))

        return lax.while_loop(lambda now: now[0] < rounds[0, 0], body, (jnp.int32(1), state))[1]

    low, high = owned[:RIM], owned[own_rows - RIM :]
    rims = swap(jnp.where(odd, high, low), jnp.where(odd, low, high))
    send, slot = pack(jnp.zeros((1, 1), i32))
    recv = exchange(send)
    first = ascend(recv, rims[0], owned, rims[1], False)
    rounds, total, words, base_of, slot_of = first[3:8]

    def more_ascent(packed, state):
        found = ascend(exchange(packed[0]), rims[0], owned, rims[1], False)
        return tuple(now + term for now, term in zip(state, found[:3]))

    grad, one, two = later_rounds(rounds, tuple(first[:3]), more_ascent)
    edges = swap(one, two)

    def last_round(packed, state):
        filler = jnp.zeros((rows - 4 * RIM, TILE), f32)
        below, above = sides(*rims)
        under, over = sides(*edges)
        atlas = jnp.concatenate([below, owned, above]) + ascent * (
            grad + jnp.concatenate([under, filler, over])
        )
        low = atlas[:RIM] * inside[0, 0]
        high = atlas[RIM + own_rows :] * inside[0, 1]
        one, two = sides(low, high)
        found = ascend(exchange(packed[0]), one, atlas[RIM : RIM + own_rows], two, True)
        return state[0] + found[0], unpack(packed[1], exchange(found[8]), state[1])

    extra, extra_correl = later_rounds(
        rounds, (jnp.zeros((rows, TILE), f32), jnp.zeros((1, tiles), f32)), last_round
    )
    atlas, slope, correl_rows = call(
        forward_kernel,
        "forward",
        [
            (total, SMEM), (base_of, SMEM), (slot_of, SMEM), (inside, SMEM), (words, VMEM),
            (owned, VMEM), (rims[0], VMEM), (rims[1], VMEM), (grad, VMEM), (edges[0], VMEM), (edges[1], VMEM),
        ],
        [((own_rows, TILE), f32, VMEM), ((room, TILE), f32, VMEM), ((groups * PAD, TILE), f32, VMEM)],
        [pltpu.VMEM((rows, TILE), f32), pltpu.VMEM((SLOTS, room, TILE), f32), pltpu.VMEM((room, TILE), f32)],
    )
    back = exchange(correl_rows)
    near, one, two = call(
        backward_kernel,
        "backward",
        [(total, SMEM), (base_of, SMEM), (inside, SMEM), (words, VMEM), (slope, VMEM), (atlas, VMEM), (extra, VMEM)],
        [((own_rows, TILE), f32, VMEM), ((RIM, TILE), f32, VMEM), ((RIM, TILE), f32, VMEM)],
        [pltpu.VMEM((room, TILE), i32), pltpu.VMEM((9, room, TILE), f32), pltpu.VMEM((rows * 8, TILE), f32)],
        30_000_000,
    )
    last = swap(one, two)
    current, correl = call(
        finish_kernel,
        "finish",
        [(inside, SMEM), (near, VMEM), (last[0], VMEM), (last[1], VMEM), (slot, VMEM), (back, VMEM), (extra_correl, VMEM)],
        [((own_rows, TILE), f32, VMEM), ((1, tiles), f32, VMEM)],
        (),
        100_000,
    )
    return (current[None], correl[None])


def solution(mesh):
    in_specs = (
        P("slab", "subj", None),
        P("subj", "slab", None, None),
        P("subj", "slab", None, None),
        P("subj", "slab", None, None, None),
        P("subj", "slab", None, None, None),
        P("subj", "slab"),
    )
    out_specs = (P("slab", "subj", None), P("subj", "slab", None))
    return jax.shard_map(shards, mesh=mesh, in_specs=in_specs, out_specs=out_specs, check_vma=False)
```

```python
import jax
import jax.numpy as jnp
from jax import lax
from jax.experimental import pallas as pl
from jax.experimental.pallas import tpu as pltpu
from jax.sharding import PartitionSpec as P

TILE = 128
SLOTS = 4
ROW = 8
ITERS = 2
HALO = 5
RIM = 8
CAP = 36
PAD = 40
META = 3 * CAP
BLOCK = 3 * CAP + 4
COUNT_AT = 126
MOST_AT = 127
FRAC_UNIT = 65535.0
U_UNIT = float(2**27)
STEP = 64
PART = 64
GROUP = 32

epsilon = 1e-05
ascent = 40.0

SPOTS = (0, 1, ROW, ROW + 1)
SHIFTS = (0, 1, 4, 5)


def pieces_of(word):
    return [
        ((word >> shift) & 255).astype(jnp.float32).astype(jnp.bfloat16) for shift in (0, 8, 16, 24)
    ]


def pack_kernel(own_rows, live_ref, round_ref, lists_ref, corners_ref, fractions_ref, subject_ref, send_ref, slot_ref):
    groups = send_ref.shape[0] // BLOCK
    tiles = subject_ref.shape[0]
    base = lists_ref[0:1, :]
    alive = lax.broadcasted_iota(jnp.int32, (1, tiles), 1) < live_ref[0, 0]
    owner = jnp.minimum(base // own_rows, groups - 1)
    local = base - owner * own_rows
    group_iota = lax.broadcasted_iota(jnp.int32, (groups, tiles), 0)
    member = jnp.where((group_iota == owner) & alive, 1.0, 0.0)
    before = lax.broadcasted_iota(jnp.int32, (tiles, tiles), 0) < lax.broadcasted_iota(
        jnp.int32, (tiles, tiles), 1
    )
    earlier = jnp.dot(
        member.astype(jnp.bfloat16),
        jnp.where(before, 1.0, 0.0).astype(jnp.bfloat16),
        preferred_element_type=jnp.float32,
    )
    counts = jnp.sum(member, axis=1, keepdims=True)
    first = round_ref[0, 0] * CAP
    rank = jnp.sum(member * earlier, axis=0, keepdims=True).astype(jnp.int32) - first
    chosen = alive & (rank >= 0) & (rank < CAP)
    slot = jnp.where(chosen, owner * PAD + rank, -1)
    slot_ref[...] = slot
    pick = jnp.where(
        lax.broadcasted_iota(jnp.int32, (groups * PAD, tiles), 0) == slot, 1.0, 0.0
    ).astype(jnp.bfloat16)

    at_rank = jnp.where(
        (lax.broadcasted_iota(jnp.int32, (TILE, tiles), 0) == rank) & chosen, 1.0, 0.0
    ).astype(jnp.bfloat16)
    local_high = (member * (local >> 4).astype(jnp.float32)).astype(jnp.bfloat16)
    local_low = (member * (local & 15).astype(jnp.float32)).astype(jnp.bfloat16)
    across = (((1,), (1,)), ((), ()))
    bases = 16.0 * lax.dot_general(
        local_high, at_rank, across, preferred_element_type=jnp.float32
    ) + lax.dot_general(local_low, at_rank, across, preferred_element_type=jnp.float32)
    here = jnp.clip(counts.astype(jnp.int32) - first, 0, CAP)
    most = jnp.max(counts, axis=0, keepdims=True).astype(jnp.int32)
    lane = lax.broadcasted_iota(jnp.int32, (groups, TILE), 1)
    header = jnp.where(
        lane == COUNT_AT, here, jnp.where(lane == MOST_AT, most, bases.astype(jnp.int32))
    )

    target = subject_ref[...].astype(jnp.float32)
    centered = target - jnp.mean(target, axis=-1, keepdims=True)
    subject_var = jnp.mean(centered * centered, axis=-1, keepdims=True) + epsilon
    unit = centered / jnp.sqrt(subject_var)
    coded = [
        (fractions_ref[d] * FRAC_UNIT + 0.5).astype(jnp.int32) for d in range(3)
    ]
    words = (
        coded[0] | (coded[1] << 16),
        coded[2] | (corners_ref[:, 0, :] << 16),
        jnp.round(unit * U_UNIT).astype(jnp.int32),
    )
    for w, word in enumerate(words):
        data = jnp.concatenate(pieces_of(word), axis=1)
        moved = jnp.dot(pick, data, preferred_element_type=jnp.float32)
        low = (moved[:, :TILE] + 256.0 * moved[:, TILE : 2 * TILE]).astype(jnp.int32)
        high = (moved[:, 2 * TILE : 3 * TILE] + 256.0 * moved[:, 3 * TILE :]).astype(jnp.int32)
        whole = low | (high << 16)
        for g in range(groups):
            send_ref[pl.ds(g * BLOCK + w * CAP, CAP), :] = whole[g * PAD : g * PAD + CAP]
    for g in range(groups):
        send_ref[pl.ds(g * BLOCK + META, 4), :] = jnp.broadcast_to(header[g : g + 1], (4, TILE))


def compact(meta_ref, groups, base_of, from_row, slot_of):
    def source(s, state):
        def take(r, place):
            base_of[place] = meta_ref[s, r] + (RIM - HALO)
            from_row[place] = s * BLOCK + r
            slot_of[place] = s * PAD + r
            return place + 1

        place = lax.fori_loop(0, meta_ref[s, COUNT_AT], take, state[0])
        return place, jnp.maximum(state[1], meta_ref[s, MOST_AT])

    total, most = lax.fori_loop(0, groups, source, (jnp.int32(0), jnp.int32(0)))
    for extra in range(GROUP):
        base_of[total + extra] = 0
        from_row[total + extra] = 0
        slot_of[total + extra] = PAD - 1
    return total, (most + (CAP - 1)) // CAP


def fetch(total, recv_ref, from_row, words, table, base_of, foot):
    def body(step, carry):
        at = pl.multiple_of(step * 8, 8)
        for i in range(8):
            here = pl.ds(at + i, 1)
            if recv_ref is not None:
                row = from_row[at + i]
                for w in range(3):
                    words[w, here, :] = recv_ref[pl.ds(row + w * CAP, 1), :]
            base = base_of[at + i]
            for k, shift in enumerate(SPOTS):
                foot[k, here, :] = table[pl.ds(base + shift, 1), :]
        return carry

    lax.fori_loop(0, (total + 7) // 8, body, 0)


def fractions_of(first, second):
    return (
        (first & 65535).astype(jnp.float32) * (1.0 / FRAC_UNIT),
        lax.shift_right_logical(first, 16).astype(jnp.float32) * (1.0 / FRAC_UNIT),
        (second & 65535).astype(jnp.float32) * (1.0 / FRAC_UNIT),
    )


def weights_of(along):
    away = [1.0 - x for x in along]
    found = []
    for q in range(8):
        weight = (
            (along[0] if q & 1 else away[0])
            * (along[1] if q & 2 else away[1])
            * (along[2] if q & 4 else away[2])
        )
        found.append(weight.astype(jnp.bfloat16).astype(jnp.float32))
    return found


def sample(total, words, foot, give):
    def piece(at):
        here = pl.ds(at, PART)
        second = words[1, here, :]
        unit = words[2, here, :].astype(jnp.float32) * (1.0 / U_UNIT)
        start = lax.shift_right_logical(second, 16)
        tables = [foot[k, here, :] for k in range(SLOTS)]
        weights = weights_of(fractions_of(words[0, here, :], second))
        peak = jnp.abs(tables[0])
        for t in tables[1:]:
            peak = jnp.maximum(peak, jnp.abs(t))
        peak = jnp.max(peak, axis=-1, keepdims=True)
        scale = jnp.where(peak > 0.0, 32767.0 / peak, 0.0)
        codes = [jnp.round(t * scale).astype(jnp.int32) for t in tables]
        couples = [(codes[k] & 65535) | (codes[k + 1] << 16) for k in (0, 2)]
        warped = None
        for q in range(8):
            column = start + (SHIFTS[q & 3] + (16 if q & 4 else 0))
            lane = column & (TILE - 1)
            got = [
                jnp.take_along_axis(c, lane, axis=1, mode="promise_in_bounds", wrap_negative_indices=False)
                for c in couples
            ]
            word = jnp.where(column < 2 * TILE, got[0], got[1])
            word = lax.shift_left(word, 16 - ((column >> 3) & 16))
            picked = lax.shift_right_arithmetic(word, jnp.full_like(word, 16)).astype(jnp.float32)
            term = weights[q] * picked
            warped = term if warped is None else warped + term
        warped = warped * (peak * (1.0 / 32767.0))
        deviation = warped - jnp.mean(warped, axis=-1, keepdims=True)
        warp_var = jnp.mean(deviation * deviation, axis=-1, keepdims=True) + epsilon
        inverse = 1.0 / jnp.sqrt(warp_var)
        correl = jnp.mean(deviation * unit, axis=-1, keepdims=True) * inverse
        slope = (unit * inverse - (correl / warp_var) * deviation) * (1.0 / TILE)
        alive = at + lax.broadcasted_iota(jnp.int32, (PART, TILE), 0) < total
        slope = jnp.where(alive, slope, 0.0).astype(jnp.bfloat16).astype(jnp.float32)
        give(here, weights, start, slope, jnp.broadcast_to(correl, (PART, TILE)))

    def body(step, carry):
        for inner in range(0, STEP, PART):
            piece(pl.multiple_of(step * STEP + inner, PART))
        return carry

    lax.fori_loop(0, (total + (STEP - 1)) // STEP, body, 0)


def send_back(total, rows, slot_of, correl_ref):
    def body(step, carry):
        at = pl.multiple_of(step * 8, 8)
        for i in range(8):
            correl_ref[pl.ds(slot_of[at + i], 1), :] = rows[pl.ds(at + i, 1), :]
        return carry

    lax.fori_loop(0, (total + 7) // 8, body, 0)


def splat_all(total, starts, values, base_of, acc):
    acc[...] = jnp.zeros(acc.shape, jnp.float32)
    high_iota = lax.broadcasted_iota(jnp.int32, (32, TILE), 0)
    low_iota = lax.broadcasted_iota(jnp.int32, (16, TILE), 0)
    across = (((1,), (1,)), ((), ()))

    def body(step, carry):
        at = pl.multiple_of(step * GROUP, GROUP)
        for i in range(GROUP):
            line = pl.ds(at + i, 1)
            start = starts[line, :]
            high = (high_iota - (start >> 4)).astype(jnp.int16)
            low = (low_iota - (start & 15)).astype(jnp.int16)
            nothing = jnp.zeros((32, TILE), jnp.bfloat16)
            slope = jnp.broadcast_to(values[8, line, :], (32, TILE)).astype(jnp.bfloat16)
            sides = [jnp.where(high == jnp.int16(j), slope, nothing) for j in range(3)]
            corner = [
                jnp.broadcast_to(values[q, line, :], (16, TILE)).astype(jnp.bfloat16) for q in range(8)
            ]
            near, far = corner[:4], corner[4:]
            inside = [low == jnp.int16(shift) for shift in SHIFTS]
            wrapped = [low == jnp.int16(shift - 16) for shift in SHIFTS]
            parts = [nothing[:16] for _ in range(3)]
            for q in range(4):
                parts[0] = jnp.where(inside[q], near[q], parts[0])
                parts[1] = jnp.where(inside[q], far[q], parts[1])
                if q > 0:
                    parts[1] = jnp.where(wrapped[q], near[q], parts[1])
                    parts[2] = jnp.where(wrapped[q], far[q], parts[2])
            splat = lax.dot_general(
                jnp.concatenate(sides, axis=1),
                jnp.concatenate(parts, axis=1),
                across,
                preferred_element_type=jnp.float32,
            )
            base = base_of[at + i]
            spots = [pl.ds(pl.multiple_of((base + shift) * 8, 8), 8) for shift in SPOTS]
            sums = [acc[spots[k], 0:16] + splat[8 * k : 8 * k + 8] for k in range(SLOTS)]
            for k in range(SLOTS):
                acc[spots[k], 0:16] = sums[k]
        return carry

    lax.fori_loop(0, (total + (GROUP - 1)) // GROUP, body, 0)


def unfold(acc, rows):
    total = None
    for j in range(8):
        line = acc[pl.ds(j, rows, stride=8), :]
        line = pltpu.roll(line, 16 * j, 1) if j else line
        total = line if total is None else total + line
    return total


def fill_table(table, below, owned, above):
    count = owned.shape[0]
    for at, value in ((0, below), (RIM, owned), (RIM + count, above)):
        table[pl.ds(at, value.shape[0]), :] = value.astype(jnp.bfloat16).astype(jnp.float32)


def ascend_kernel(
    back, meta_ref, inside_ref, recv_ref, owned_ref, first_ref, second_ref,
    grad_ref, one_ref, two_ref, rounds_ref, total_ref, words, base_of, slot_of, correl_ref,
    table, foot, starts, values, acc, from_row,
):
    groups = recv_ref.shape[0] // BLOCK
    rows = grad_ref.shape[0]
    odd = inside_ref[0, 2] > 0.0
    one, two = first_ref[...], second_ref[...]
    fill_table(table, jnp.where(odd, two, one), owned_ref[...], jnp.where(odd, one, two))
    total, rounds = compact(meta_ref, groups, base_of, from_row, slot_of)
    rounds_ref[0, 0] = rounds
    total_ref[0, 0] = total
    fetch(total, recv_ref, from_row, words, table, base_of, foot)

    def give(here, weights, start, slope, correl):
        starts[here, :] = start
        for q in range(8):
            values[q, here, :] = weights[q]
        values[8, here, :] = slope
        if back:
            values[9, here, :] = correl

    sample(total, words, foot, give)
    if back:
        send_back(total, values.at[9], slot_of, correl_ref)
    splat_all(total, starts, values, base_of, acc)
    grad = unfold(acc, rows)
    grad_ref[...] = grad
    low, high = grad[: 2 * RIM], grad[rows - 2 * RIM :]
    one_ref[...] = jnp.where(odd, high, low)
    two_ref[...] = jnp.where(odd, low, high)


def forward_kernel(
    total_ref, base_of, slot_of, inside_ref, words, owned_ref, first_ref, second_ref, grad_ref, one_ref, two_ref,
    atlas_ref, slope_ref, correl_ref,
    table, foot, marks,
):
    own_rows = owned_ref.shape[0]
    rows = own_rows + 2 * RIM
    total = total_ref[0, 0]
    odd = inside_ref[0, 2] > 0.0
    one, two = one_ref[...], two_ref[...]
    first = grad_ref[0 : 2 * RIM, :] + jnp.where(odd, two, one)
    last = grad_ref[rows - 2 * RIM : rows, :] + jnp.where(odd, one, two)
    one, two = first_ref[...], second_ref[...]
    below = (jnp.where(odd, two, one) + ascent * first[:RIM]) * inside_ref[0, 0]
    above = (jnp.where(odd, one, two) + ascent * last[RIM:]) * inside_ref[0, 1]
    atlas_ref[0:RIM, :] = owned_ref[0:RIM, :] + ascent * first[RIM:]
    atlas_ref[RIM : own_rows - RIM, :] = (
        owned_ref[RIM : own_rows - RIM, :] + ascent * grad_ref[2 * RIM : own_rows, :]
    )
    atlas_ref[own_rows - RIM : own_rows, :] = owned_ref[own_rows - RIM : own_rows, :] + ascent * last[:RIM]
    fill_table(table, below, atlas_ref[...], above)
    fetch(total, None, None, None, table, base_of, foot)

    def give(here, weights, start, slope, correl):
        slope_ref[here, :] = slope
        marks[here, :] = correl

    sample(total, words, foot, give)
    send_back(total, marks, slot_of, correl_ref)


def backward_kernel(
    total_ref, base_of, inside_ref, words, slope_ref, atlas_ref, extra_ref,
    near_ref, one_ref, two_ref,
    starts, values, acc,
):
    own_rows = atlas_ref.shape[0]
    rows = own_rows + 2 * RIM
    total = total_ref[0, 0]

    def spread(step, carry):
        here = pl.ds(pl.multiple_of(step * STEP, STEP), STEP)
        second = words[1, here, :]
        values[8, here, :] = slope_ref[here, :]
        starts[here, :] = lax.shift_right_logical(second, 16)
        for q, weight in enumerate(weights_of(fractions_of(words[0, here, :], second))):
            values[q, here, :] = weight
        return carry

    lax.fori_loop(0, (total + (STEP - 1)) // STEP, spread, 0)
    splat_all(total, starts, values, base_of, acc)
    grad = unfold(acc, rows) + extra_ref[...]
    odd = inside_ref[0, 2] > 0.0
    low, high = grad[:RIM], grad[rows - RIM :]
    one_ref[...] = jnp.where(odd, high, low)
    two_ref[...] = jnp.where(odd, low, high)
    near_ref[...] = atlas_ref[...] + ascent * grad[RIM : RIM + own_rows]


def unpack_kernel(slot_ref, back_ref, extra_ref, correl_ref):
    slot = slot_ref[...]
    tiles = slot.shape[1]
    total = jnp.zeros((PAD, tiles), jnp.float32)
    inner = lax.broadcasted_iota(jnp.int32, (PAD, tiles), 0)
    for g in range(back_ref.shape[0] // PAD):
        block = back_ref[pl.ds(g * PAD, PAD), :]
        wide = jnp.concatenate([block] * (tiles // TILE), axis=1)
        total = total + jnp.where(inner == slot - g * PAD, wide, 0.0)
    correl_ref[...] = jnp.sum(total, axis=0, keepdims=True) + extra_ref[...]


def finish_kernel(
    inside_ref, near_ref, one_ref, two_ref, slot_ref, back_ref, extra_ref, atlas_ref, correl_ref
):
    odd = inside_ref[0, 2] > 0.0
    one, two = one_ref[...], two_ref[...]
    atlas_ref[...] = near_ref[...]
    atlas_ref[0:RIM, :] += ascent * jnp.where(odd, two, one)
    rows = atlas_ref.shape[0]
    atlas_ref[rows - RIM : rows, :] += ascent * jnp.where(odd, one, two)
    unpack_kernel(slot_ref, back_ref, extra_ref, correl_ref)


VMEM = pl.BlockSpec(memory_space=pltpu.VMEM)
SMEM = pl.BlockSpec(memory_space=pltpu.SMEM)
LIMIT = pltpu.CompilerParams(vmem_limit_bytes=48 * 1024 * 1024)


def shards(template, subject, tile_lists, corners, fractions, live_tiles):
    groups = lax.axis_size("subj")
    slabs = lax.axis_size("slab")
    owned = template[0]
    own_rows = owned.shape[0]
    tiles = subject.shape[2]
    rows = own_rows + 2 * RIM
    room = (groups * CAP + STEP) // STEP * STEP
    planes = jnp.transpose(fractions[0, 0], (1, 0, 2))
    f32, i32 = jnp.float32, jnp.int32

    def call(kernel, name, inputs, outputs, scratch=(), cost=3_000_000):
        return pl.pallas_call(
            kernel,
            out_shape=[jax.ShapeDtypeStruct(shape, kind) for shape, kind, _ in outputs],
            in_specs=[space for _, space in inputs],
            out_specs=[space for _, _, space in outputs],
            scratch_shapes=list(scratch),
            compiler_params=LIMIT,
            cost_estimate=pl.CostEstimate(flops=0, bytes_accessed=cost, transcendentals=0),
            name=name,
        )(*[value for value, _ in inputs])

    count = groups * slabs
    order = [(k % groups) * slabs + k // groups for k in range(count)]
    both = ("subj", "slab")
    place = lax.axis_index("slab") * groups + lax.axis_index("subj")
    odd = place % 2 == 1
    inside = jnp.stack([place > 0, place < count - 1, odd]).astype(f32).reshape(1, 3)

    def pairs_from(start):
        found = [(order[k], order[k + 1]) for k in range(start, count - 1, 2)]
        return found + [(there, here) for here, there in found]

    def swap(one, two):
        return lax.ppermute(one, both, pairs_from(1)), lax.ppermute(two, both, pairs_from(0))

    def sides(one, two):
        return jnp.where(odd, two, one), jnp.where(odd, one, two)

    def pack(number):
        def kernel(*refs):
            pack_kernel(own_rows, *refs)

        return call(
            kernel,
            "pack",
            [(live_tiles, SMEM), (number, SMEM), (tile_lists[0, 0], VMEM), (corners[0, 0], VMEM), (planes, VMEM), (subject[0, 0], VMEM)],
            [((groups * BLOCK, TILE), i32, VMEM), ((1, tiles), i32, VMEM)],
        )

    def exchange(send):
        return lax.all_to_all(send, "subj", 0, 0, tiled=True)

    def ascend(recv, one, owned, two, back):
        meta = recv.reshape(groups, BLOCK, TILE)[:, META, :]

        def kernel(*refs):
            ascend_kernel(back, *refs)

        return call(
            kernel,
            "ascend",
            [(meta, SMEM), (inside, SMEM), (recv, VMEM), (owned, VMEM), (one, VMEM), (two, VMEM)],
            [
                ((rows, TILE), f32, VMEM),
                ((2 * RIM, TILE), f32, VMEM),
                ((2 * RIM, TILE), f32, VMEM),
                ((1, 1), i32, SMEM),
                ((1, 1), i32, SMEM),
                ((3, room, TILE), i32, VMEM),
                ((room,), i32, SMEM),
                ((room,), i32, SMEM),
                ((groups * PAD if back else 8, TILE), f32, VMEM),
            ],
            [
                pltpu.VMEM((rows, TILE), f32),
                pltpu.VMEM((SLOTS, room, TILE), f32),
                pltpu.VMEM((room, TILE), i32),
                pltpu.VMEM((10, room, TILE), f32),
                pltpu.VMEM((rows * 8, TILE), f32),
                pltpu.SMEM((room,), i32),
            ],
        )

    def unpack(slot, back, extra):
        return call(
            unpack_kernel,
            "unpack",
            [(slot, VMEM), (back, VMEM), (extra, VMEM)],
            [((1, tiles), f32, VMEM)],
        )[0]

    def later_rounds(later, state, work):
        def body(now):
            return (now[0] - 1, work(pack(now[0].reshape(1, 1)), now[1]))

        return lax.while_loop(lambda now: now[0] > 0, body, (later, state))[1]

    low, high = owned[:RIM], owned[own_rows - RIM :]
    rims = swap(jnp.where(odd, high, low), jnp.where(odd, low, high))
    send, slot = pack(jnp.zeros((1, 1), i32))
    recv = exchange(send)
    first = ascend(recv, rims[0], owned, rims[1], False)
    rounds, total, words, base_of, slot_of = first[3:8]
    later = rounds[0, 0] - 1

    def more_ascent(packed, state):
        found = ascend(exchange(packed[0]), rims[0], owned, rims[1], False)
        return tuple(now + term for now, term in zip(state, found[:3]))

    grad, one, two = later_rounds(later, tuple(first[:3]), more_ascent)
    edges = swap(one, two)

    def last_round(packed, state):
        filler = jnp.zeros((rows - 4 * RIM, TILE), f32)
        below, above = sides(*rims)
        under, over = sides(*edges)
        atlas = jnp.concatenate([below, owned, above]) + ascent * (
            grad + jnp.concatenate([under, filler, over])
        )
        low = atlas[:RIM] * inside[0, 0]
        high = atlas[RIM + own_rows :] * inside[0, 1]
        one, two = sides(low, high)
        found = ascend(exchange(packed[0]), one, atlas[RIM : RIM + own_rows], two, True)
        return state[0] + found[0], unpack(packed[1], exchange(found[8]), state[1])

    extra, extra_correl = later_rounds(
        later, (jnp.zeros((rows, TILE), f32), jnp.zeros((1, tiles), f32)), last_round
    )
    atlas, slope, correl_rows = call(
        forward_kernel,
        "forward",
        [
            (total, SMEM), (base_of, SMEM), (slot_of, SMEM), (inside, SMEM), (words, VMEM),
            (owned, VMEM), (rims[0], VMEM), (rims[1], VMEM), (grad, VMEM), (edges[0], VMEM), (edges[1], VMEM),
        ],
        [((own_rows, TILE), f32, VMEM), ((room, TILE), f32, VMEM), ((groups * PAD, TILE), f32, VMEM)],
        [pltpu.VMEM((rows, TILE), f32), pltpu.VMEM((SLOTS, room, TILE), f32), pltpu.VMEM((room, TILE), f32)],
    )
    back = exchange(correl_rows)
    near, one, two = call(
        backward_kernel,
        "backward",
        [(total, SMEM), (base_of, SMEM), (inside, SMEM), (words, VMEM), (slope, VMEM), (atlas, VMEM), (extra, VMEM)],
        [((own_rows, TILE), f32, VMEM), ((RIM, TILE), f32, VMEM), ((RIM, TILE), f32, VMEM)],
        [pltpu.VMEM((room, TILE), i32), pltpu.VMEM((9, room, TILE), f32), pltpu.VMEM((rows * 8, TILE), f32)],
        30_000_000,
    )
    last = swap(one, two)
    current, correl = call(
        finish_kernel,
        "finish",
        [(inside, SMEM), (near, VMEM), (last[0], VMEM), (last[1], VMEM), (slot, VMEM), (back, VMEM), (extra_correl, VMEM)],
        [((own_rows, TILE), f32, VMEM), ((1, tiles), f32, VMEM)],
        (),
        100_000,
    )
    return (current[None], correl[None])


def solution(mesh):
    in_specs = (
        P("slab", "subj", None),
        P("subj", "slab", None, None),
        P("subj", "slab", None, None),
        P("subj", "slab", None, None, None),
        P("subj", "slab", None, None, None),
        P("subj", "slab"),
    )
    out_specs = (P("slab", "subj", None), P("subj", "slab", None))
    return jax.shard_map(shards, mesh=mesh, in_specs=in_specs, out_specs=out_specs, check_vma=False)
```
